512 devices in a mesh: tm: 128 (over y, z, core), space: 4 (over x).
Axes of the slice: x: 4, y: 8, z: 8, core: 2. Of those that a mesh axis runs over, the one named last changes fastest.
Arguments:
- u_coarse_guess: float32 [1024, 32, 1024], P('tm', 'space'), may hold values from -6 to 6
- forcing: float32 [2048, 32, 1024], P('tm', 'space'), may hold values from -6 to 6
- u_init: float32 [32, 1024], P('space'), may hold values from -6 to 6
- diffuse: float32 [32, 1024], P('space'), may hold values from 0.01 to 0.03
- vel_x: float32 [32, 1024], P('space'), may hold values from -0.05 to 0.05
- vel_y: float32 [32, 1024], P('space'), may hold values from -0.05 to 0.05
- react: float32 [32, 1024], P('space'), may hold values from 0.0002 to 0.02
Outputs:
- u_next: float32 [2048, 32, 1024], P('tm', 'space')
The draws below stay inside these ranges and needn't reach their ends.
All inputs are finite; a program needn't handle non-finite values.
Results may differ from the reference program's by a relative error of at most 0.00013.
Values sent between devices are 32-bit elements; how exact they have to be, the bound alone decides.
A program may use at most 64 MiB of HBM per device.

```python
import math
import jax
import jax.numpy as jnp
from jax import lax

COLS = 1024
NT = 2048
NR = 32


def levels(stream_key, extent, split, low, top_value):
    factor_of, own = 1.0, jax.random.fold_in(stream_key, 6)
    for position, blocks in split:
        heights = jnp.exp(jax.random.uniform(jax.random.fold_in(own, position), (blocks,), jnp.float32, low / len(split), top_value / len(split)))
        factor_of = factor_of * jnp.repeat(heights, extent[position] // blocks).reshape([-1 if axis == position else 1 for axis in range(len(extent))])
    return factor_of


def bell_draw(rng, dims, scale, most, shards=(), dtype=jnp.bfloat16):
    entries = scale * jax.random.normal(rng, dims, jnp.float32)
    if shards:
        entries = entries * levels(rng, dims, shards, -0.22, 0.18)
    return jnp.clip(entries, -most, most).astype(dtype)


def setup_inputs(seed: int = 0) -> dict:
    key_list = jax.random.split(jax.random.key(seed), 8)
    u_coarse_guess = bell_draw(key_list[0], (NT // 2, NR, COLS), 1.0, 6.0, ((0, 128), (1, 4)), jnp.float32)
    forcing = bell_draw(key_list[1], (NT, NR, COLS), 1.0, 6.0, ((0, 128), (1, 4)), jnp.float32)
    u_init = bell_draw(key_list[2], (NR, COLS), 1.0, 6.0, ((0, 4),), jnp.float32)
    diffuse = jnp.clip(0.01 + 0.02 * jax.random.uniform(key_list[3], (NR, COLS), jnp.float32) ** levels(key_list[3], (NR, COLS), ((0, 4),), -0.2, 0.2), 0.01, 0.03)
    vel_x = jnp.clip(jax.random.uniform(key_list[4], (NR, COLS), jnp.float32, -0.05, 0.05) * levels(key_list[4], (NR, COLS), ((0, 4),), -0.4, 0.0), -0.05, 0.05)
    vel_y = jnp.clip(jax.random.uniform(key_list[5], (NR, COLS), jnp.float32, -0.05, 0.05) * levels(key_list[5], (NR, COLS), ((0, 4),), -0.4, 0.0), -0.05, 0.05)
    react = jnp.clip(jnp.exp(math.log(0.02) - 4.6051702 * jax.random.uniform(key_list[6], (NR, COLS), jnp.float32) ** levels(key_list[6], (NR, COLS), ((0, 4),), -0.2, 0.2)), 0.0002, 0.02)
    return dict(u_coarse_guess=u_coarse_guess, forcing=forcing, u_init=u_init, diffuse=diffuse, vel_x=vel_x, vel_y=vel_y, react=react)


def stencil_terms(diffuse, vel_x, vel_y, react):
    west_term = diffuse + jnp.maximum(vel_x, 0.0)
    east_term = diffuse - jnp.minimum(vel_x, 0.0)
    north_term = diffuse + jnp.maximum(vel_y, 0.0)
    south_term = diffuse - jnp.minimum(vel_y, 0.0)
    centre = -(4.0 * diffuse + jnp.abs(vel_x) + jnp.abs(vel_y) + react)
    return (west_term, east_term, north_term, south_term, centre)


def advance_padded(padded, terms, factor):
    west_term, east_term, north_term, south_term, centre = terms
    centre_val = padded[..., 1:-1, :]
    north_val = padded[..., :-2, :]
    south_val = padded[..., 2:, :]
    blank_col = jnp.zeros_like(centre_val[..., :1])
    west_val = jnp.concatenate([blank_col, centre_val[..., :-1]], axis=-1)
    east_val = jnp.concatenate([centre_val[..., 1:], blank_col], axis=-1)
    change = centre * centre_val + west_term * west_val + east_term * east_val + north_term * north_val + south_term * south_val
    return centre_val + factor * change


def advance_all(stack, terms, factor):
    def single(field):
        blank_row = jnp.zeros_like(field[:1])
        return advance_padded(jnp.concatenate([blank_row, field, blank_row], axis=0), terms, factor)
    return lax.map(single, stack)


def reference(u_coarse_guess, forcing, u_init, diffuse, vel_x, vel_y, react):
    terms = stencil_terms(diffuse, vel_x, vel_y, react)
    decay = jnp.exp(-8.0 * react)
    rows, cols = u_init.shape
    force = forcing.reshape(-1, 2, rows, cols)
    force_fine = force[:, 0]
    force_coarse = force[:, 1]
    start = u_init[None]
    u_fine = advance_all(jnp.concatenate([start, u_coarse_guess[:-1]], axis=0), terms, 1.0) + force_fine
    u_coarse = advance_all(u_fine, terms, 1.0) + force_coarse
    u_fine = advance_all(jnp.concatenate([start, u_coarse[:-1]], axis=0), terms, 1.0) + force_fine
    resid_one = advance_all(u_fine, terms, 1.0) + force_coarse - u_coarse
    resid_two = advance_all(resid_one[0::2], terms, 2.0) + resid_one[1::2]
    resid_three = advance_all(resid_two[0::2], terms, 4.0) + resid_two[1::2]

    def chain(carried, resid):
        fresh = decay * carried + resid
        return fresh, fresh

    final_state, err_three = lax.scan(chain, jnp.zeros_like(u_init), resid_three)
    blank = jnp.zeros_like(u_init)[None]
    earlier = jnp.concatenate([blank, err_three[:-1]], axis=0)
    err_two_fine = advance_all(earlier, terms, 4.0) + resid_two[0::2]
    err_two = jnp.stack([err_two_fine, err_three], axis=1).reshape(-1, rows, cols)
    earlier_two = jnp.concatenate([blank, err_two[:-1]], axis=0)
    err_one_fine = advance_all(earlier_two, terms, 2.0) + resid_one[0::2]
    err_one = jnp.stack([err_one_fine, err_two], axis=1).reshape(-1, rows, cols)
    u_coarse = u_coarse + err_one
    u_fine = advance_all(jnp.concatenate([start, u_coarse[:-1]], axis=0), terms, 1.0) + force_fine
    return jnp.stack([u_fine, u_coarse], axis=1).reshape(forcing.shape)
```

```python
import functools

import jax
import jax.numpy as jnp
from jax import lax
from jax.experimental import pallas as pl
from jax.experimental.pallas import tpu as pltpu
from jax.sharding import PartitionSpec as P

MESH = pl.DeviceIdType.MESH
GROUP = 16
PAD = 8
DEPTH = 6


def add_squares(x):
    zero = None
    out = []
    for m in range(len(x) + 2):
        terms = []
        if m < len(x):
            terms.append(x[m])
        if 1 <= m <= len(x):
            terms.append(2.0 * x[m - 1])
        if 2 <= m <= len(x) + 1:
            terms.append(x[m - 2])
        total = terms[0]
        for t in terms[1:]:
            total = total + t
        out.append(total)
    del zero
    return out


def kernel(
    slabs,
    strips,
    guess,
    force,
    init,
    diffuse,
    vel_x,
    vel_y,
    react,
    out,
    gx,
    fx,
    hx,
    cx,
    wx,
    decx,
    px,
    dx,
    zx,
    rx,
    tx,
    ex,
    ob,
    ini,
    g7,
    d7,
    sp,
    dp,
    r1,
    pre,
    pw,
    r2,
    wo,
    ce,
    cex,
    lsem,
    es,
    er,
    ss,
    sr,
):
    tm = lax.axis_index("tm")
    sx = lax.axis_index("space")
    y = tm // GROUP
    q = lax.rem(tm, GROUP)
    count = slabs * GROUP
    xs = (lax.rem(sx + 1, strips), lax.rem(sx + strips - 1, strips))
    nxt = lax.rem(tm + 1, count)
    prv = lax.rem(tm + count - 1, count)
    last = tm == count - 1
    cols = ob.shape[2]
    own = pl.ds(PAD, 8)

    barrier = pltpu.get_barrier_semaphore()
    peers = [(tm, s) for s in xs]
    for t in (nxt, prv):
        peers += [(t, s) for s in (sx,) + xs]
    for m in range(1, GROUP):
        t = y * GROUP + lax.rem(q + m, GROUP)
        peers += [(t, s) for s in (sx,) + xs]
    for m in range(1, slabs):
        peers.append((lax.rem(y + m, slabs) * GROUP + q, sx))
    for dev in peers:
        pl.semaphore_signal(barrier, inc=1, device_id=dev, device_id_type=MESH)

    loads = []
    for i, (src, dst) in enumerate(
        [
            (guess, gx.at[pl.ds(1, 8), own]),
            (force.at[:, 0], fx.at[:, own]),
            (force.at[:, 1], hx),
            (init, ini),
            (diffuse, cx.at[0, own]),
            (vel_x, cx.at[1, own]),
            (vel_y, cx.at[2, own]),
            (react, cx.at[3, own]),
        ]
    ):
        cp = pltpu.make_async_copy(src, dst, lsem.at[i])
        cp.start()
        loads.append(cp)
    for cp in loads:
        cp.wait()

    sent = []
    slot = [0]

    def send(src, dst, dev):
        i = slot[0]
        slot[0] += 1
        cp = pltpu.make_async_remote_copy(
            src_ref=src,
            dst_ref=dst,
            send_sem=ss.at[i],
            recv_sem=sr.at[i],
            device_id=dev,
            device_id_type=MESH,
        )
        cp.start()
        sent.append(cp)
        return cp

    def halo(ref, lead, h):
        a = send(ref.at[lead + (pl.ds(16 - h, h),)], ref.at[lead + (pl.ds(8 - h, h),)], (tm, xs[0]))
        b = send(ref.at[lead + (pl.ds(8, h),)], ref.at[lead + (pl.ds(16, h),)], (tm, xs[1]))
        return [a, b]

    def onward(src, ref, lead, h):
        return [
            send(src, ref.at[lead + (own,)], (nxt, sx)),
            send(src.at[pl.ds(8 - h, h)], ref.at[lead + (pl.ds(8 - h, h),)], (nxt, xs[0])),
            send(src.at[pl.ds(0, h)], ref.at[lead + (pl.ds(16, h),)], (nxt, xs[1])),
        ]

    def change(G, F, H, k):
        return (G[k - 1] + F[k] + H[k] - G[k], 2.0 * G[k - 1] + F[k], G[k - 1])

    def reader(ref, lane, shift, padded):
        def read(k):
            if padded:
                return ref[k + shift, own, lane]
            return ref[k + shift, :, lane]

        class Reader:
            def __getitem__(self, k):
                return read(k)

        return Reader()

    def fields(lane):
        return reader(gx, lane, 1, True), reader(fx, lane, 0, True), reader(hx, lane, 0, False)

    def first(lane):
        G, F, H = fields(lane)
        d0, d1, d2 = [jnp.where(last, 0.0, v) for v in change(G, F, H, 7)]
        g = jnp.where(last, ini[:, lane], G[7])
        g7[:, lane] = g
        return [
            d0 + g,
            d1 + 6.0 * (d0 + g),
            d2 + 6.0 * d1 + 8.0 * d0 + 9.0 * g,
            6.0 * d2 + 8.0 * d1 + 4.0 * g,
            8.0 * d2,
        ]

    def second(lane):
        G, F, H = fields(lane)
        a0, a1, a2 = change(G, F, H, 3)
        b0, b1, b2 = change(G, F, H, 4)
        c0, c1, c2 = change(G, F, H, 5)
        e0, e1, e2 = change(G, F, H, 6)
        return [
            a0 + b0 + c0 + e0,
            a1 + 6.0 * a0 + b1 + 4.0 * b0 + c1 + 2.0 * c0 + e1,
            a2 + 6.0 * a1 + 8.0 * a0 + b2 + 4.0 * b1 + c2 + 2.0 * c1 + e2,
            6.0 * a2 + 8.0 * a1 + 4.0 * b2 + 2.0 * c2,
            8.0 * a2,
        ]

    def third(lane):
        G, F, H = fields(lane)
        b1 = F[0]
        b0 = b1 + H[0] - G[0]
        c0, c1, c2 = change(G, F, H, 1)
        e0, e1, e2 = change(G, F, H, 2)
        return [
            b0 + c0 + e0,
            b1 + 4.0 * b0 + c1 + 2.0 * c0 + e1,
            4.0 * b1 + c2 + 2.0 * c1 + e2,
            2.0 * c2,
        ]

    def combine(p, make):
        def one(j, carry):
            lane = pl.ds(pl.multiple_of(j * 128, 128), 128)
            for m, v in enumerate(add_squares(make(lane))):
                px[p, m, own, lane] = v
            return carry

        lax.fori_loop(0, cols // 128, one, 0)

    def power(p, m, side):
        h = m
        if side == 0:
            src, dst, dev = pl.ds(16 - h, h), pl.ds(8 - h, h), (tm, xs[0])
        else:
            src, dst, dev = pl.ds(8, h), pl.ds(16, h), (tm, xs[1])
        return pltpu.make_async_remote_copy(
            src_ref=px.at[p, m, src],
            dst_ref=px.at[p, m, dst],
            send_sem=es.at[p, m - 1, side],
            recv_sem=er.at[p, m - 1, side],
            device_id=dev,
            device_id_type=MESH,
        )

    def send_powers(p, top):
        for m in range(top, 0, -1):
            for side in (0, 1):
                power(p, m, side).start()

    combine(0, first)
    pl.semaphore_wait(barrier, len(peers))

    coef = halo(cx, (slice(None),), 5)
    send_powers(0, DEPTH)
    combine(1, second)
    send_powers(1, DEPTH)
    combine(2, third)
    px[2, DEPTH] = jnp.zeros_like(px[2, DEPTH])
    send_powers(2, DEPTH - 1)
    early = halo(gx, (pl.ds(1, 7),), 2) + halo(fx, (slice(None),), 1) + onward(g7, gx, (0,), 2)

    for cp in coef:
        cp.wait_recv()

    def weights(t, carry):
        rows = pl.ds(pl.multiple_of(t * 8, 8), 8)
        dif, vx, vy, rea = cx[0, rows], cx[1, rows], cx[2, rows], cx[3, rows]
        row = lax.broadcasted_iota(jnp.int32, dif.shape, 0) + t * 8
        col = lax.broadcasted_iota(jnp.int32, dif.shape, 1)
        top = (row == PAD) & (sx == 0)
        bottom = (row == PAD + 7) & (sx == strips - 1)
        wx[0, rows] = jnp.where(col == 0, 0.0, dif + jnp.maximum(vx, 0.0))
        wx[1, rows] = jnp.where(col == cols - 1, 0.0, dif - jnp.minimum(vx, 0.0))
        wx[2, rows] = jnp.where(top, 0.0, dif + jnp.maximum(vy, 0.0))
        wx[3, rows] = jnp.where(bottom, 0.0, dif - jnp.minimum(vy, 0.0))
        wx[4, rows] = -(4.0 * dif + jnp.abs(vx) + jnp.abs(vy) + rea)
        decx[rows] = jnp.exp(-8.0 * rea)
        return carry

    lax.fori_loop(0, 3, weights, 0)

    def ap(v):
        n = v.shape[0]
        return (
            wx[4] * v
            + wx[0] * pltpu.roll(v, 1, 1)
            + wx[1] * pltpu.roll(v, cols - 1, 1)
            + wx[2] * pltpu.roll(v, 1, 0)
            + wx[3] * pltpu.roll(v, n - 1, 0)
        )

    def mid(v):
        return v[PAD : PAD + 8]

    def horner(p, carry):
        @pl.when(p < 2)
        def _():
            for side in (0, 1):
                power(p, DEPTH, side).wait_recv()

        for m in range(DEPTH - 1, 0, -1):
            for side in (0, 1):
                power(p, m, side).wait_recv()

        def level(i, v):
            return ap(v) + px[p, DEPTH - 1 - i]

        v = lax.fori_loop(0, DEPTH, level, px[p, DEPTH])
        rx[p, own] = mid(v)
        return carry

    lax.fori_loop(0, 3, horner, 0)

    dec = decx[own]
    first_value = rx[0, own]
    part = jnp.where(last, first_value, dec * (dec * rx[2, own] + rx[1, own]) + first_value)
    for h in (0, 1):
        for j in range(8):
            sp[8 * h + j] = part[4 * h : 4 * h + 4, 128 * j : 128 * j + 128]
            dp[8 * h + j] = dec[4 * h : 4 * h + 4, 128 * j : 128 * j + 128]

    scatter = []
    for m in range(1, GROUP):
        to = lax.rem(q + m, GROUP)
        scatter.append(send(sp.at[to], r1.at[q], (y * GROUP + to, sx)))
    r1[q] = sp[q]
    d1 = dp[q]
    d2 = d1 * d1

    for cp in early:
        cp.wait_recv()

    def changes(k, carry):
        g, f = gx[k], fx[k]
        v = ap(g) + 2.0 * g + f
        dx[k + 1, own] = mid(ap(v)) + mid(g + f) + hx[k] - gx[k + 1, own]
        return carry

    lax.fori_loop(0, 8, changes, 0)
    d7[...] = jnp.where(last, 0.0, dx[8, own])
    middle = []
    for k, h in ((0, 3), (1, 2), (3, 4), (4, 3), (5, 2)):
        middle += halo(dx, (k + 1,), h)
    middle += onward(d7, dx, (0,), 4)
    late = halo(rx, (2,), 3) + onward(rx.at[0, own], tx, (), 3)

    for cp in scatter:
        cp.wait_recv()
    acc = jnp.zeros_like(d2)
    fac = jnp.ones_like(d2)
    for i in range(GROUP):
        pre[i] = acc
        pw[i] = fac
        acc = d2 * acc + r1[i]
        fac = d2 * fac
    r2[y] = jnp.where(y == slabs - 1, r1[GROUP - 1], acc)
    across = []
    for m in range(1, slabs):
        to = lax.rem(y + m, slabs)
        across.append(send(r2.at[y], r2.at[y], (to * GROUP + q, sx)))

    for cp in middle:
        cp.wait_recv()
    zx[0] = gx[0] + dx[0]

    def twice(v):
        v = v + ap(v)
        return mid(v) + mid(ap(v))

    def blocks(b, carry):
        k = 4 * b
        a = dx[k]
        bb = dx[k + 1]
        c = dx[k + 2]
        zx[k + 1, own] = gx[k + 1, own] + mid(bb) + twice(a)
        w = a + 2.0 * ap(a) + bb
        zx[k + 2, own] = gx[k + 2, own] + mid(c) + twice(w)
        w = w + 2.0 * ap(w) + c
        zx[k + 3, own] = gx[k + 3, own] + dx[k + 3, own] + twice(w)
        zx[k + 4, own] = gx[k + 4, own] + dx[k + 4, own]
        return carry

    lax.fori_loop(0, 2, blocks, 0)
    coarse = halo(zx, (pl.ds(1, 7),), 1)

    for cp in across:
        cp.wait_recv()
    acc = r2[slabs - 1]
    for i in range(slabs - 1):
        acc = jnp.where(i < y, fac * acc + r2[i], acc)
    for i in range(GROUP):
        wo[i] = pw[i] * acc + pre[i]
    half = q // 8
    tile = lax.rem(q, 8)
    side = lax.rem(sx + 2 * half + strips - 1, strips)
    gather = []
    for m in range(GROUP):
        to = lax.rem(q + m, GROUP)
        dev = y * GROUP + to
        if m:
            gather.append(send(wo.at[to], ce.at[tile, 1 + half], (dev, sx)))
        gather.append(send(wo.at[to], ce.at[tile, 3 - 3 * half], (dev, side)))
    ce[tile, 1 + half] = wo[q]

    for cp in coarse:
        cp.wait_recv()

    def results(k, carry):
        v = zx[k]
        ob[2 * k] = mid(v) + mid(ap(v)) + fx[k, own]
        ob[2 * k + 1] = zx[k + 1, own]
        return carry

    lax.fori_loop(0, 8, results, 0)
    for cp in late:
        cp.wait_recv()

    for cp in gather:
        cp.wait_recv()
    for j in range(8):
        lane = pl.ds(128 * j, 128)
        for quarter in range(4):
            cex[pl.ds(4 + 4 * quarter, 4), lane] = ce[j, quarter]
    v = cex[...]
    w = v + rx[2]
    ex[0] = (v - tx[...]) * jnp.exp(8.0 * cx[3])
    ex[1] = w
    ex[2, own] = mid(decx[...] * w) + rx[1, own]
    stores = []

    def finish(b, carry):
        e = ex[b]
        a1 = ap(e)
        a2 = ap(a1)
        a3 = mid(ap(a2))
        e, a1, a2 = mid(e), mid(a1), mid(a2)
        k = 8 * b
        ob[k] += e + a1
        ob[k + 1] += e + 2.0 * a1
        ob[k + 2] += e + 3.0 * a1 + 2.0 * a2
        ob[k + 3] += e + 4.0 * a1
        ob[k + 4] += e + 5.0 * a1 + 4.0 * a2
        ob[k + 5] += e + 6.0 * a1 + 8.0 * a2
        ob[k + 6] += e + 7.0 * a1 + 14.0 * a2 + 8.0 * a3
        ob[k + 7] += ex[b + 1, own]
        pltpu.make_async_copy(ob.at[pl.ds(k, 8)], out.at[pl.ds(k, 8)], lsem.at[b]).start()
        return carry

    lax.fori_loop(0, 2, finish, 0)
    for b in range(2):
        pltpu.make_async_copy(ob.at[pl.ds(8 * b, 8)], out.at[pl.ds(8 * b, 8)], lsem.at[b]).wait()
    for cp in sent:
        cp.wait_send()
    for p in range(3):
        for m in range(1, DEPTH + 1 - p // 2):
            for s in (0, 1):
                power(p, m, s).wait_send()


def body(slabs, strips, u_coarse_guess, forcing, u_init, diffuse, vel_x, vel_y, react):
    points, rows, cols = u_coarse_guess.shape
    wide = rows + 2 * PAD
    copies = 2 + 4 + 3 + 15 + 10 + 3 + 2 + 3 + 7 + 2 + 31
    f32 = jnp.float32

    def vmem(*shape):
        return pltpu.VMEM(shape, f32)

    return pl.pallas_call(
        functools.partial(kernel, slabs, strips),
        out_shape=jax.ShapeDtypeStruct(forcing.shape, f32),
        in_specs=[pl.BlockSpec(memory_space=pl.ANY)] * 7,
        out_specs=pl.BlockSpec(memory_space=pl.ANY),
        scratch_shapes=[
            vmem(points + 1, wide, cols),
            vmem(points, wide, cols),
            vmem(points, rows, cols),
            vmem(4, wide, cols),
            vmem(5, wide, cols),
            vmem(wide, cols),
            vmem(3, DEPTH + 1, wide, cols),
            vmem(points + 1, wide, cols),
            vmem(points + 1, wide, cols),
            vmem(3, wide, cols),
            vmem(wide, cols),
            vmem(3, wide, cols),
            vmem(2 * points, rows, cols),
            vmem(rows, cols),
            vmem(rows, cols),
            vmem(rows, cols),
            vmem(GROUP, 4, 128),
            vmem(GROUP, 4, 128),
            vmem(GROUP, 4, 128),
            vmem(GROUP, 4, 128),
            vmem(GROUP, 4, 128),
            vmem(slabs, 4, 128),
            vmem(GROUP, 4, 128),
            vmem(8, 4, 4, 128),
            vmem(wide, cols),
            pltpu.SemaphoreType.DMA((8,)),
            pltpu.SemaphoreType.DMA((3, DEPTH, 2)),
            pltpu.SemaphoreType.DMA((3, DEPTH, 2)),
            pltpu.SemaphoreType.DMA((copies,)),
            pltpu.SemaphoreType.DMA((copies,)),
        ],
        compiler_params=pltpu.CompilerParams(
            collective_id=0, has_side_effects=True, vmem_limit_bytes=32 << 20
        ),
        cost_estimate=pl.CostEstimate(flops=10_000_000, bytes_accessed=1_500_000, transcendentals=16384),
    )(
        u_coarse_guess,
        forcing.reshape(points, 2, rows, cols),
        u_init,
        diffuse,
        vel_x,
        vel_y,
        react,
    )


def solution(mesh):
    slabs = mesh.shape["tm"] // GROUP
    strips = mesh.shape["space"]
    whole = P("tm", "space", None)
    row = P("space", None)
    return jax.shard_map(
        functools.partial(body, slabs, strips),
        mesh=mesh,
        in_specs=(whole, whole) + (row,) * 5,
        out_specs=whole,
        check_vma=False,
    )
```

```python
import functools

import jax
import jax.numpy as jnp
from jax import lax
from jax.experimental import pallas as pl
from jax.experimental.pallas import tpu as pltpu
from jax.sharding import PartitionSpec as P

MESH = pl.DeviceIdType.MESH
GROUP = 16
PAD = 8
DEPTH = 6


def add_squares(x):
    out = []
    for m in range(len(x) + 2):
        terms = []
        if m < len(x):
            terms.append(x[m])
        if 1 <= m <= len(x):
            terms.append(2.0 * x[m - 1])
        if 2 <= m <= len(x) + 1:
            terms.append(x[m - 2])
        total = terms[0]
        for t in terms[1:]:
            total = total + t
        out.append(total)
    return out


def kernel(
    slabs,
    strips,
    guess,
    force,
    init,
    diffuse,
    vel_x,
    vel_y,
    react,
    out,
    gx,
    fx,
    hx,
    cx,
    wx,
    decx,
    px,
    dx,
    zx,
    rx,
    qx,
    fp,
    tx,
    ex,
    ob,
    ini,
    g7,
    d7,
    sp,
    dp,
    r1,
    pre,
    pw,
    r2,
    wo,
    ce,
    ch,
    cex,
    lsem,
    ss,
    sr,
):
    tm = lax.axis_index("tm")
    sx = lax.axis_index("space")
    y = tm // GROUP
    q = lax.rem(tm, GROUP)
    count = slabs * GROUP
    xs = (lax.rem(sx + 1, strips), lax.rem(sx + strips - 1, strips))
    nxt = lax.rem(tm + 1, count)
    prv = lax.rem(tm + count - 1, count)
    last = tm == count - 1
    cols = ob.shape[2]
    own = pl.ds(PAD, 8)

    barrier = pltpu.get_barrier_semaphore()
    peers = [(tm, s) for s in xs]
    for t in (nxt, prv):
        peers += [(t, s) for s in (sx,) + xs]
    for m in range(1, GROUP):
        t = y * GROUP + lax.rem(q + m, GROUP)
        peers += [(t, s) for s in (sx,) + xs]
    for m in range(1, slabs):
        peers.append((lax.rem(y + m, slabs) * GROUP + q, sx))
    for dev in peers:
        pl.semaphore_signal(barrier, inc=1, device_id=dev, device_id_type=MESH)

    loads = []
    for i, (src, dst) in enumerate(
        [
            (guess, gx.at[pl.ds(1, 8), own]),
            (force.at[:, 0], fx.at[:, own]),
            (force.at[:, 1], hx),
            (init, ini),
            (diffuse, cx.at[0, own]),
            (vel_x, cx.at[1, own]),
            (vel_y, cx.at[2, own]),
            (react, cx.at[3, own]),
        ]
    ):
        cp = pltpu.make_async_copy(src, dst, lsem.at[i])
        cp.start()
        loads.append(cp)
    for cp in loads:
        cp.wait()

    sent = []
    slot = [0]

    def send(src, dst, dev):
        i = slot[0]
        slot[0] += 1
        cp = pltpu.make_async_remote_copy(
            src_ref=src,
            dst_ref=dst,
            send_sem=ss.at[i],
            recv_sem=sr.at[i],
            device_id=dev,
            device_id_type=MESH,
        )
        cp.start()
        sent.append(cp)
        return cp

    class Batch:
        def __init__(self, items, whole):
            i = slot[0]
            slot[0] += 1
            for src, dst, dev in items:
                self.copy = pltpu.make_async_remote_copy(
                    src_ref=src,
                    dst_ref=dst,
                    send_sem=ss.at[i],
                    recv_sem=sr.at[i],
                    device_id=dev,
                    device_id_type=MESH,
                )
                self.copy.start()
            self.total = pltpu.make_async_remote_copy(
                src_ref=whole,
                dst_ref=whole,
                send_sem=ss.at[i],
                recv_sem=sr.at[i],
                device_id=items[0][2],
                device_id_type=MESH,
            )
            sent.append(self.total)

        def wait_recv(self):
            self.total.wait_recv()

    def far_first(n):
        return sorted(range(1, n), key=lambda m: -min(m, n - m))

    def halo(ref, lead, h):
        a = send(ref.at[lead + (pl.ds(16 - h, h),)], ref.at[lead + (pl.ds(8 - h, h),)], (tm, xs[0]))
        b = send(ref.at[lead + (pl.ds(8, h),)], ref.at[lead + (pl.ds(16, h),)], (tm, xs[1]))
        return [a, b]

    def onward(src, ref, lead, h):
        return [
            send(src, ref.at[lead + (own,)], (nxt, sx)),
            send(src.at[pl.ds(8 - h, h)], ref.at[lead + (pl.ds(8 - h, h),)], (nxt, xs[0])),
            send(src.at[pl.ds(0, h)], ref.at[lead + (pl.ds(16, h),)], (nxt, xs[1])),
        ]

    def change(G, F, H, k):
        return (G[k - 1] + F[k] + H[k] - G[k], 2.0 * G[k - 1] + F[k], G[k - 1])

    def reader(ref, lane, shift, padded):
        def read(k):
            if padded:
                return ref[k + shift, own, lane]
            return ref[k + shift, :, lane]

        class Reader:
            def __getitem__(self, k):
                return read(k)

        return Reader()

    def fields(lane):
        return reader(gx, lane, 1, True), reader(fx, lane, 0, True), reader(hx, lane, 0, False)

    def first(lane):
        G, F, H = fields(lane)
        d0, d1, d2 = [jnp.where(last, 0.0, v) for v in change(G, F, H, 7)]
        g = jnp.where(last, ini[:, lane], G[7])
        g7[:, lane] = g
        return [
            d0 + g,
            d1 + 6.0 * (d0 + g),
            d2 + 6.0 * d1 + 8.0 * d0 + 9.0 * g,
            6.0 * d2 + 8.0 * d1 + 4.0 * g,
            8.0 * d2,
        ]

    def second(lane):
        G, F, H = fields(lane)
        a0, a1, a2 = change(G, F, H, 3)
        b0, b1, b2 = change(G, F, H, 4)
        c0, c1, c2 = change(G, F, H, 5)
        e0, e1, e2 = change(G, F, H, 6)
        return [
            a0 + b0 + c0 + e0,
            a1 + 6.0 * a0 + b1 + 4.0 * b0 + c1 + 2.0 * c0 + e1,
            a2 + 6.0 * a1 + 8.0 * a0 + b2 + 4.0 * b1 + c2 + 2.0 * c1 + e2,
            6.0 * a2 + 8.0 * a1 + 4.0 * b2 + 2.0 * c2,
            8.0 * a2,
        ]

    def third(lane):
        G, F, H = fields(lane)
        b1 = F[0]
        b0 = b1 + H[0] - G[0]
        c0, c1, c2 = change(G, F, H, 1)
        e0, e1, e2 = change(G, F, H, 2)
        return [
            b0 + c0 + e0,
            b1 + 4.0 * b0 + c1 + 2.0 * c0 + e1,
            4.0 * b1 + c2 + 2.0 * c1 + e2,
            2.0 * c2,
        ]

    def combine(p, make):
        def one(j, carry):
            lane = pl.ds(pl.multiple_of(j * 128, 128), 128)
            for m, v in enumerate(add_squares(make(lane))):
                px[p, m, :, lane] = v
            return carry

        lax.fori_loop(0, cols // 128, one, 0)

    pl.semaphore_wait(barrier, len(peers))
    coef = halo(cx, (slice(None),), DEPTH)
    early = halo(gx, (pl.ds(1, 7),), 2) + halo(fx, (slice(None),), 1)
    combine(0, first)
    early += onward(g7, gx, (0,), 2)
    combine(1, second)
    combine(2, third)

    for cp in coef:
        cp.wait_recv()

    def weights(t, carry):
        rows = pl.ds(pl.multiple_of(t * 8, 8), 8)
        dif, vx, vy, rea = cx[0, rows], cx[1, rows], cx[2, rows], cx[3, rows]
        row = lax.broadcasted_iota(jnp.int32, dif.shape, 0) + t * 8
        col = lax.broadcasted_iota(jnp.int32, dif.shape, 1)
        inside = (row >= PAD - DEPTH) & (row < PAD + 8 + DEPTH)
        inside &= (row >= PAD) | (sx > 0)
        inside &= (row < PAD + 8) | (sx < strips - 1)
        top = (row == PAD) & (sx == 0)
        bottom = (row == PAD + 7) & (sx == strips - 1)
        west = jnp.where(col == 0, 0.0, dif + jnp.maximum(vx, 0.0))
        east = jnp.where(col == cols - 1, 0.0, dif - jnp.minimum(vx, 0.0))
        north = jnp.where(top, 0.0, dif + jnp.maximum(vy, 0.0))
        south = jnp.where(bottom, 0.0, dif - jnp.minimum(vy, 0.0))
        centre = -(4.0 * dif + jnp.abs(vx) + jnp.abs(vy) + rea)
        for i, v in enumerate((west, east, north, south, centre)):
            wx[i, rows] = jnp.where(inside, v, 0.0)
        decx[rows] = jnp.where(inside, jnp.exp(-8.0 * rea), 0.0)
        return carry

    lax.fori_loop(0, 3, weights, 0)

    def ap(v):
        n = v.shape[0]
        return (
            wx[4] * v
            + wx[0] * pltpu.roll(v, 1, 1)
            + wx[1] * pltpu.roll(v, cols - 1, 1)
            + wx[2] * pltpu.roll(v, 1, 0)
            + wx[3] * pltpu.roll(v, n - 1, 0)
        )

    def mid(v):
        return v[PAD : PAD + 8]

    def around(v):
        none = jnp.zeros_like(v)
        return jnp.concatenate([none, v, none], axis=0)

    def horner(p, carry):
        top = DEPTH - p // 2

        def level(i, v):
            return ap(v) + around(px[p, top - 1 - i])

        rx[p] = lax.fori_loop(0, top, level, around(px[p, top]))
        return carry

    lax.fori_loop(0, 3, horner, 0)

    decv = decx[...]
    dec = mid(decv)
    value = rx[0]
    part = jnp.where(last, value, decv * (decv * rx[2] + rx[1]) + value)
    for h in (0, 1):
        for j in range(8):
            dp[8 * h + j] = dec[4 * h : 4 * h + 4, 128 * j : 128 * j + 128]
            for t in range(3):
                r = 8 * t + 4 * h
                sp[t, 8 * h + j] = part[r : r + 4, 128 * j : 128 * j + 128]

    def mate(m):
        to = lax.rem(q + m, GROUP)
        return to, y * GROUP + to

    items = ([], [], [])
    for m in far_first(GROUP) + [0]:
        to, dev = mate(m)
        items[2].append((sp.at[2, to], r1.at[2, q], (dev, xs[0])))
        items[0].append((sp.at[0, to], r1.at[0, q], (dev, xs[1])))
        if m:
            items[1].append((sp.at[1, to], r1.at[1, q], (dev, sx)))
    scatter = [Batch(items[2], r1.at[2]), Batch(items[0], r1.at[0]), Batch(items[1], r1.at[1, pl.ds(0, GROUP - 1)])]
    r1[1, q] = sp[1, q]
    spill = [
        send(rx.at[:, pl.ds(16, DEPTH)], qx.at[0, :, pl.ds(0, DEPTH)], (tm, xs[0])),
        send(rx.at[:, pl.ds(8 - DEPTH, DEPTH)], qx.at[1, :, pl.ds(8 - DEPTH, DEPTH)], (tm, xs[1])),
    ]
    d1 = dp[q]
    d2 = d1 * d1

    for cp in early:
        cp.wait_recv()

    def changes(k, carry):
        g, f = gx[k], fx[k]
        v = ap(g) + 2.0 * g + f
        dx[k + 1, own] = mid(ap(v)) + mid(g + f) + hx[k] - gx[k + 1, own]
        return carry

    lax.fori_loop(0, 8, changes, 0)
    d7[...] = jnp.where(last, 0.0, dx[8, own])
    middle = []
    for k, h in ((0, 3), (1, 2), (3, 4), (4, 3), (5, 2)):
        middle += halo(dx, (k + 1,), h)
    middle += onward(d7, dx, (0,), 4)
    for cp in spill:
        cp.wait_recv()
    row = lax.broadcasted_iota(jnp.int32, (8, cols), 0)
    for p in range(3):
        above = jnp.where(row < DEPTH, qx[0, p], 0.0)
        below = jnp.where(row >= 8 - DEPTH, qx[1, p], 0.0)
        fp[p, own] = rx[p, own] + above + below
    late = halo(fp, (2,), 3) + onward(fp.at[0, own], tx, (), 3)

    for cp in scatter:
        cp.wait_recv()
    acc = jnp.zeros_like(d2)
    fac = jnp.ones_like(d2)
    for i in range(GROUP):
        pre[i] = acc
        pw[i] = fac
        part = r1[1, i] + r1[2, i] + r1[0, i]
        acc = d2 * acc + part
        fac = d2 * fac
    r2[y] = jnp.where(y == slabs - 1, part, acc)
    items = []
    for m in far_first(slabs):
        items.append((r2.at[y], r2.at[y], (lax.rem(y + m, slabs) * GROUP + q, sx)))
    across = [Batch(items, r2.at[pl.ds(0, slabs - 1)])]

    for cp in middle:
        cp.wait_recv()
    zx[0] = gx[0] + dx[0]

    def twice(v):
        v = v + ap(v)
        return mid(v) + mid(ap(v))

    def blocks(b, carry):
        k = 4 * b
        a = dx[k]
        bb = dx[k + 1]
        c = dx[k + 2]
        zx[k + 1, own] = gx[k + 1, own] + mid(bb) + twice(a)
        w = a + 2.0 * ap(a) + bb
        zx[k + 2, own] = gx[k + 2, own] + mid(c) + twice(w)
        w = w + 2.0 * ap(w) + c
        zx[k + 3, own] = gx[k + 3, own] + dx[k + 3, own] + twice(w)
        zx[k + 4, own] = gx[k + 4, own] + dx[k + 4, own]
        return carry

    lax.fori_loop(0, 2, blocks, 0)
    coarse = halo(zx, (pl.ds(1, 7),), 1)

    for cp in across:
        cp.wait_recv()
    acc = r2[slabs - 1]
    for i in range(slabs - 1):
        acc = jnp.where(i < y, fac * acc + r2[i], acc)
    for i in range(GROUP):
        wo[i] = pw[i] * acc + pre[i]
    half = q // 8
    side = lax.rem(sx + 2 * half + strips - 1, strips)
    items = ([], [])
    for m in far_first(GROUP) + [0]:
        to, dev = mate(m)
        items[0].append((wo.at[to], ch.at[q], (dev, side)))
        if m:
            items[1].append((wo.at[to], ce.at[q], (dev, sx)))
    early_sent = list(sent)
    gather = [Batch(items[0], ch), Batch(items[1], ce.at[pl.ds(0, GROUP - 1)])]
    ce[q] = wo[q]

    for cp in coarse:
        cp.wait_recv()

    def results(k, carry):
        v = zx[k]
        ob[2 * k] = mid(v) + mid(ap(v)) + fx[k, own]
        ob[2 * k + 1] = zx[k + 1, own]
        return carry

    lax.fori_loop(0, 8, results, 0)
    for cp in late:
        cp.wait_recv()
    for cp in early_sent:
        cp.wait_send()

    for cp in gather:
        cp.wait_recv()
    for j in range(8):
        lane = pl.ds(128 * j, 128)
        cex[4:8, lane] = ch[8 + j]
        cex[8:12, lane] = ce[j]
        cex[12:16, lane] = ce[8 + j]
        cex[16:20, lane] = ch[j]
    v = cex[...]
    w = v + fp[2]
    ex[0] = (v - tx[...]) * jnp.exp(8.0 * cx[3])
    ex[1] = w
    ex[2, own] = mid(decx[...] * w) + fp[1, own]
    stores = []

    def finish(b, carry):
        e = ex[b]
        a1 = ap(e)
        a2 = ap(a1)
        a3 = mid(ap(a2))
        e, a1, a2 = mid(e), mid(a1), mid(a2)
        k = 8 * b
        ob[k] += e + a1
        ob[k + 1] += e + 2.0 * a1
        ob[k + 2] += e + 3.0 * a1 + 2.0 * a2
        ob[k + 3] += e + 4.0 * a1
        ob[k + 4] += e + 5.0 * a1 + 4.0 * a2
        ob[k + 5] += e + 6.0 * a1 + 8.0 * a2
        ob[k + 6] += e + 7.0 * a1 + 14.0 * a2 + 8.0 * a3
        ob[k + 7] += ex[b + 1, own]
        pltpu.make_async_copy(ob.at[pl.ds(k, 8)], out.at[pl.ds(k, 8)], lsem.at[b]).start()
        return carry

    lax.fori_loop(0, 2, finish, 0)
    for b in range(2):
        pltpu.make_async_copy(ob.at[pl.ds(8 * b, 8)], out.at[pl.ds(8 * b, 8)], lsem.at[b]).wait()
    for cp in gather:
        cp.total.wait_send()


def body(slabs, strips, u_coarse_guess, forcing, u_init, diffuse, vel_x, vel_y, react):
    points, rows, cols = u_coarse_guess.shape
    wide = rows + 2 * PAD
    copies = 2 + 4 + 3 + 3 + 2 + 10 + 3 + 2 + 3 + 1 + 2 + 2
    f32 = jnp.float32

    def vmem(*shape):
        return pltpu.VMEM(shape, f32)

    return pl.pallas_call(
        functools.partial(kernel, slabs, strips),
        out_shape=jax.ShapeDtypeStruct(forcing.shape, f32),
        in_specs=[pl.BlockSpec(memory_space=pltpu.HBM)] * 7,
        out_specs=pl.BlockSpec(memory_space=pl.ANY),
        scratch_shapes=[
            vmem(points + 1, wide, cols),
            vmem(points, wide, cols),
            vmem(points, rows, cols),
            vmem(4, wide, cols),
            vmem(5, wide, cols),
            vmem(wide, cols),
            vmem(3, DEPTH + 1, rows, cols),
            vmem(points + 1, wide, cols),
            vmem(points + 1, wide, cols),
            vmem(3, wide, cols),
            vmem(2, 3, rows, cols),
            vmem(3, wide, cols),
            vmem(wide, cols),
            vmem(3, wide, cols),
            vmem(2 * points, rows, cols),
            vmem(rows, cols),
            vmem(rows, cols),
            vmem(rows, cols),
            vmem(3, GROUP, 4, 128),
            vmem(GROUP, 4, 128),
            vmem(3, GROUP, 4, 128),
            vmem(GROUP, 4, 128),
            vmem(GROUP, 4, 128),
            vmem(slabs, 4, 128),
            vmem(GROUP, 4, 128),
            vmem(GROUP, 4, 128),
            vmem(GROUP, 4, 128),
            vmem(wide, cols),
            pltpu.SemaphoreType.DMA((8,)),
            pltpu.SemaphoreType.DMA((copies,)),
            pltpu.SemaphoreType.DMA((copies,)),
        ],
        compiler_params=pltpu.CompilerParams(
            collective_id=0, has_side_effects=True, vmem_limit_bytes=60 << 20
        ),
        cost_estimate=pl.CostEstimate(flops=10_000_000, bytes_accessed=1_500_000, transcendentals=16384),
    )(
        u_coarse_guess,
        forcing.reshape(points, 2, rows, cols),
        u_init,
        diffuse,
        vel_x,
        vel_y,
        react,
    )


def solution(mesh):
    slabs = mesh.shape["tm"] // GROUP
    strips = mesh.shape["space"]
    whole = P("tm", "space", None)
    row = P("space", None)
    return jax.shard_map(
        functools.partial(body, slabs, strips),
        mesh=mesh,
        in_specs=(whole, whole) + (row,) * 5,
        out_specs=whole,
        check_vma=False,
    )
```

```python
import functools

import jax
import jax.numpy as jnp
from jax import lax
from jax.experimental import pallas as pl
from jax.experimental.pallas import tpu as pltpu
from jax.sharding import PartitionSpec as P

MESH = pl.DeviceIdType.MESH
GROUP = 16
PAD = 8
NEAR = 4
DEPTH = 6


def add_squares(x):
    out = []
    for m in range(len(x) + 2):
        terms = []
        if m < len(x):
            terms.append(x[m])
        if 1 <= m <= len(x):
            terms.append(2.0 * x[m - 1])
        if 2 <= m <= len(x) + 1:
            terms.append(x[m - 2])
        total = terms[0]
        for t in terms[1:]:
            total = total + t
        out.append(total)
    return out


def kernel(
    slabs,
    strips,
    guess,
    force,
    init,
    diffuse,
    vel_x,
    vel_y,
    react,
    ob,
    gx,
    fx,
    hx,
    cx,
    cn,
    cf,
    wx,
    wn,
    inv,
    rn,
    decx,
    px,
    dx,
    zx,
    rx,
    qx,
    fp,
    tx,
    ex,
    ini,
    g7,
    d7,
    sp,
    dp,
    r1,
    pre,
    pw,
    r2,
    wo,
    ce,
    ch,
    cex,
    lsem,
    ss,
    sr,
):
    tm = lax.axis_index("tm")
    sx = lax.axis_index("space")
    y = tm // GROUP
    q = lax.rem(tm, GROUP)
    count = slabs * GROUP
    xs = (lax.rem(sx + 1, strips), lax.rem(sx + strips - 1, strips))
    nxt = lax.rem(tm + 1, count)
    prv = lax.rem(tm + count - 1, count)
    last = tm == count - 1
    cols = ob.shape[2]
    own = pl.ds(0, 8)
    centre_rows = pl.ds(PAD, 8)

    barrier = pltpu.get_barrier_semaphore()
    peers = [(tm, s) for s in xs]
    for t in (nxt, prv):
        peers += [(t, s) for s in (sx,) + xs]
    for m in range(1, GROUP):
        t = y * GROUP + lax.rem(q + m, GROUP)
        peers += [(t, s) for s in (sx,) + xs]
    for m in range(1, slabs):
        peers.append((lax.rem(y + m, slabs) * GROUP + q, sx))
    for dev in peers:
        pl.semaphore_signal(barrier, inc=1, device_id=dev, device_id_type=MESH)

    loads = []
    for i, (src, dst) in enumerate(
        [
            (guess, gx.at[pl.ds(1, 8), own]),
            (force.at[:, 0], fx.at[:, own]),
            (force.at[:, 1], hx),
            (init, ini),
            (diffuse, cx.at[0]),
            (vel_x, cx.at[1]),
            (vel_y, cx.at[2]),
            (react, cx.at[3]),
        ]
    ):
        cp = pltpu.make_async_copy(src, dst, lsem.at[i])
        cp.start()
        loads.append(cp)
    for cp in loads:
        cp.wait()

    sent = []
    slot = [0]

    def send(src, dst, dev):
        i = slot[0]
        slot[0] += 1
        cp = pltpu.make_async_remote_copy(
            src_ref=src,
            dst_ref=dst,
            send_sem=ss.at[i],
            recv_sem=sr.at[i],
            device_id=dev,
            device_id_type=MESH,
        )
        cp.start()
        sent.append(cp)
        return cp

    class Batch:
        def __init__(self, items, whole):
            i = slot[0]
            slot[0] += 1
            for src, dst, dev in items:
                self.copy = pltpu.make_async_remote_copy(
                    src_ref=src,
                    dst_ref=dst,
                    send_sem=ss.at[i],
                    recv_sem=sr.at[i],
                    device_id=dev,
                    device_id_type=MESH,
                )
                self.copy.start()
            self.total = pltpu.make_async_remote_copy(
                src_ref=whole,
                dst_ref=whole,
                send_sem=ss.at[i],
                recv_sem=sr.at[i],
                device_id=items[0][2],
                device_id_type=MESH,
            )
            sent.append(self.total)

        def wait_recv(self):
            self.total.wait_recv()

    def far_first(n):
        return sorted(range(1, n), key=lambda m: -min(m, n - m))

    def halo(ref, lead, h):
        a = send(ref.at[lead + (pl.ds(8 - h, h),)], ref.at[lead + (pl.ds(16 - h, h),)], (tm, xs[0]))
        b = send(ref.at[lead + (pl.ds(0, h),)], ref.at[lead + (pl.ds(8, h),)], (tm, xs[1]))
        return [a, b]

    def onward(src, ref, lead, h):
        return [
            send(src, ref.at[lead + (own,)], (nxt, sx)),
            send(src.at[pl.ds(8 - h, h)], ref.at[lead + (pl.ds(16 - h, h),)], (nxt, xs[0])),
            send(src.at[pl.ds(0, h)], ref.at[lead + (pl.ds(8, h),)], (nxt, xs[1])),
        ]

    def change(G, F, H, k):
        return (G[k - 1] + F[k] + H[k] - G[k], 2.0 * G[k - 1] + F[k], G[k - 1])

    def reader(ref, lane, shift, padded):
        def read(k):
            if padded:
                return ref[k + shift, own, lane]
            return ref[k + shift, :, lane]

        class Reader:
            def __getitem__(self, k):
                return read(k)

        return Reader()

    def fields(lane):
        return reader(gx, lane, 1, True), reader(fx, lane, 0, True), reader(hx, lane, 0, False)

    def first(lane):
        G, F, H = fields(lane)
        d0, d1, d2 = [jnp.where(last, 0.0, v) for v in change(G, F, H, 7)]
        g = jnp.where(last, ini[:, lane], G[7])
        g7[:, lane] = g
        return [
            d0 + g,
            d1 + 6.0 * (d0 + g),
            d2 + 6.0 * d1 + 8.0 * d0 + 9.0 * g,
            6.0 * d2 + 8.0 * d1 + 4.0 * g,
            8.0 * d2,
        ]

    def second(lane):
        G, F, H = fields(lane)
        a0, a1, a2 = change(G, F, H, 3)
        b0, b1, b2 = change(G, F, H, 4)
        c0, c1, c2 = change(G, F, H, 5)
        e0, e1, e2 = change(G, F, H, 6)
        return [
            a0 + b0 + c0 + e0,
            a1 + 6.0 * a0 + b1 + 4.0 * b0 + c1 + 2.0 * c0 + e1,
            a2 + 6.0 * a1 + 8.0 * a0 + b2 + 4.0 * b1 + c2 + 2.0 * c1 + e2,
            6.0 * a2 + 8.0 * a1 + 4.0 * b2 + 2.0 * c2,
            8.0 * a2,
        ]

    def third(lane):
        G, F, H = fields(lane)
        b1 = F[0]
        b0 = b1 + H[0] - G[0]
        c0, c1, c2 = change(G, F, H, 1)
        e0, e1, e2 = change(G, F, H, 2)
        return [
            b0 + c0 + e0,
            b1 + 4.0 * b0 + c1 + 2.0 * c0 + e1,
            4.0 * b1 + c2 + 2.0 * c1 + e2,
            2.0 * c2,
        ]

    def combine(p, make):
        def one(j, carry):
            lane = pl.ds(pl.multiple_of(j * 128, 128), 128)
            for m, v in enumerate(add_squares(make(lane))):
                px[p, m, :, lane] = v
            return carry

        lax.fori_loop(0, cols // 128, one, 0)

    pl.semaphore_wait(barrier, len(peers))

    def parameters(dst, up, down, n):
        return [
            send(cx.at[:, pl.ds(up, n)], dst.at[:, pl.ds(up, n)], (tm, xs[0])),
            send(cx.at[:, pl.ds(down, n)], dst.at[:, pl.ds(down, n)], (tm, xs[1])),
        ]

    near = parameters(cn, 8 - NEAR, 0, NEAR)
    far = parameters(cf, 8 - DEPTH, NEAR, DEPTH - NEAR)
    early = halo(gx, (pl.ds(1, 7),), 2) + halo(fx, (slice(None),), 1)
    combine(0, first)
    early += onward(g7, gx, (0,), 2)
    combine(1, second)
    combine(2, third)

    row = lax.broadcasted_iota(jnp.int32, (8, cols), 0)
    col = lax.broadcasted_iota(jnp.int32, (8, cols), 1)
    low = row < NEAR
    above = sx > 0
    beneath = sx < strips - 1

    def weights(raw, inside, top, bottom):
        dif, vx, vy, rea = raw
        west = jnp.where(col == 0, 0.0, dif + jnp.maximum(vx, 0.0))
        east = jnp.where(col == cols - 1, 0.0, dif - jnp.minimum(vx, 0.0))
        north = dif + jnp.maximum(vy, 0.0)
        south = dif - jnp.minimum(vy, 0.0)
        centre = -(4.0 * dif + jnp.abs(vx) + jnp.abs(vy) + rea)
        if inside is not None:
            return [jnp.where(inside, v, 0.0) for v in (west, east, north, south, centre)]
        return [west, east, jnp.where(top, 0.0, north), jnp.where(bottom, 0.0, south), centre]

    raw = [cx[i] for i in range(4)]
    edge = weights(raw, None, (row == 0) & (sx == 0), (row == 7) & (sx == strips - 1))
    for i, v in enumerate(edge):
        wx[i, 8:16] = v
        wn[i, 0:8] = v
    decx[8:16] = jnp.exp(-8.0 * raw[3])
    inv[0:8] = jnp.exp(8.0 * raw[3])

    for cp in near:
        cp.wait_recv()
    raw = [cn[i] for i in range(4)]
    for i, v in enumerate(weights(raw, (low & beneath) | (~low & above), None, None)):
        wn[i, 8:16] = v
    inv[8:16] = jnp.exp(8.0 * raw[3])

    def stencil(w, v):
        n = v.shape[0]
        return (
            w[4] * v
            + w[0] * pltpu.roll(v, 1, 1)
            + w[1] * pltpu.roll(v, cols - 1, 1)
            + w[2] * pltpu.roll(v, 1, 0)
            + w[3] * pltpu.roll(v, n - 1, 0)
        )

    def ap(v):
        return stencil(wn, v)

    def mid(v):
        return v[0:8]

    def around(v):
        none = jnp.zeros_like(v)
        return jnp.concatenate([none, v, none], axis=0)

    def horner_near(p, carry):
        top = DEPTH - p // 2

        def start(m):
            v = px[p, m]
            return jnp.concatenate([v, jnp.zeros_like(v)], axis=0)

        def level(i, v):
            return ap(v) + start(top - 1 - i)

        rn[p] = lax.fori_loop(0, NEAR, level, start(top))
        return carry

    lax.fori_loop(0, 3, horner_near, 0)

    for cp in far:
        cp.wait_recv()
    for t, inside in ((0, (row >= PAD - DEPTH) & above), (2, (row < DEPTH) & beneath)):
        raw = [jnp.where(low, cn[i] if t else cf[i], cf[i] if t else cn[i]) for i in range(4)]
        for i, v in enumerate(weights(raw, inside, None, None)):
            wx[i, 8 * t : 8 * t + 8] = v
        decx[8 * t : 8 * t + 8] = jnp.where(inside, jnp.exp(-8.0 * raw[3]), 0.0)

    def horner_far(p, carry):
        top = DEPTH - p // 2

        def level(i, v):
            return stencil(wx, v) + around(px[p, top - 1 - NEAR - i])

        v = rn[p, 8:16]
        v = jnp.concatenate([jnp.where(low, 0.0, v), rn[p, 0:8], jnp.where(low, v, 0.0)], axis=0)
        rx[p] = lax.fori_loop(0, top - NEAR, level, v)
        return carry

    lax.fori_loop(0, 3, horner_far, 0)

    decv = decx[...]
    dec = decv[8:16]
    value = rx[0]
    part = jnp.where(last, value, decv * (decv * rx[2] + rx[1]) + value)
    for h in (0, 1):
        for j in range(8):
            dp[8 * h + j] = dec[4 * h : 4 * h + 4, 128 * j : 128 * j + 128]
            for t in range(3):
                r = 8 * t + 4 * h
                sp[t, 8 * h + j] = part[r : r + 4, 128 * j : 128 * j + 128]

    def mate(m):
        to = lax.rem(q + m, GROUP)
        return to, y * GROUP + to

    items = ([], [], [])
    for m in far_first(GROUP) + [0]:
        to, dev = mate(m)
        items[2].append((sp.at[2, to], r1.at[2, q], (dev, xs[0])))
        items[0].append((sp.at[0, to], r1.at[0, q], (dev, xs[1])))
        if m:
            items[1].append((sp.at[1, to], r1.at[1, q], (dev, sx)))
    scatter = [Batch(items[2], r1.at[2]), Batch(items[0], r1.at[0]), Batch(items[1], r1.at[1, pl.ds(0, GROUP - 1)])]
    r1[1, q] = sp[1, q]
    spill = [
        send(rx.at[:, pl.ds(16, DEPTH)], qx.at[0, :, pl.ds(0, DEPTH)], (tm, xs[0])),
        send(rx.at[:, pl.ds(8 - DEPTH, DEPTH)], qx.at[1, :, pl.ds(8 - DEPTH, DEPTH)], (tm, xs[1])),
    ]
    d1 = dp[q]
    d2 = d1 * d1

    for cp in early:
        cp.wait_recv()

    def changes(k, carry):
        g, f = gx[k], fx[k]
        v = ap(g) + 2.0 * g + f
        dx[k + 1, own] = mid(ap(v)) + mid(g + f) + hx[k] - gx[k + 1, own]
        return carry

    lax.fori_loop(0, 8, changes, 0)
    d7[...] = jnp.where(last, 0.0, dx[8, own])
    middle = []
    for k, h in ((0, 3), (1, 2), (3, 4), (4, 3), (5, 2)):
        middle += halo(dx, (k + 1,), h)
    middle += onward(d7, dx, (0,), 4)
    for cp in spill:
        cp.wait_recv()
    for p in range(3):
        over = jnp.where(row < DEPTH, qx[0, p], 0.0)
        under = jnp.where(row >= 8 - DEPTH, qx[1, p], 0.0)
        fp[p, own] = rx[p, centre_rows] + over + under
    late = halo(fp, (2,), 3) + onward(fp.at[0, own], tx, (), 3)

    for cp in scatter:
        cp.wait_recv()
    acc = jnp.zeros_like(d2)
    fac = jnp.ones_like(d2)
    for i in range(GROUP):
        pre[i] = acc
        pw[i] = fac
        part = r1[1, i] + r1[2, i] + r1[0, i]
        acc = d2 * acc + part
        fac = d2 * fac
    r2[y] = jnp.where(y == slabs - 1, part, acc)
    items = []
    for m in far_first(slabs):
        items.append((r2.at[y], r2.at[y], (lax.rem(y + m, slabs) * GROUP + q, sx)))
    across = [Batch(items, r2.at[pl.ds(0, slabs - 1)])]

    for cp in middle:
        cp.wait_recv()
    zx[0] = gx[0] + dx[0]

    def twice(v):
        v = v + ap(v)
        return mid(v) + mid(ap(v))

    def blocks(b, carry):
        k = 4 * b
        a = dx[k]
        bb = dx[k + 1]
        c = dx[k + 2]
        zx[k + 1, own] = gx[k + 1, own] + mid(bb) + twice(a)
        w = a + 2.0 * ap(a) + bb
        zx[k + 2, own] = gx[k + 2, own] + mid(c) + twice(w)
        w = w + 2.0 * ap(w) + c
        zx[k + 3, own] = gx[k + 3, own] + dx[k + 3, own] + twice(w)
        zx[k + 4, own] = gx[k + 4, own] + dx[k + 4, own]
        return carry

    lax.fori_loop(0, 2, blocks, 0)
    coarse = halo(zx, (pl.ds(1, 7),), 1)

    for cp in across:
        cp.wait_recv()
    acc = r2[slabs - 1]
    for i in range(slabs - 1):
        acc = jnp.where(i < y, fac * acc + r2[i], acc)
    for i in range(GROUP):
        wo[i] = pw[i] * acc + pre[i]
    half = q // 8
    side = lax.rem(sx + 2 * half + strips - 1, strips)
    items = ([], [])
    for m in far_first(GROUP) + [0]:
        to, dev = mate(m)
        items[0].append((wo.at[to], ch.at[q], (dev, side)))
        if m:
            items[1].append((wo.at[to], ce.at[q], (dev, sx)))
    early_sent = list(sent)
    gather = [Batch(items[0], ch), Batch(items[1], ce.at[pl.ds(0, GROUP - 1)])]
    ce[q] = wo[q]

    for cp in coarse:
        cp.wait_recv()

    def results(k, carry):
        v = zx[k]
        ob[2 * k] = mid(v) + mid(ap(v)) + fx[k, own]
        ob[2 * k + 1] = zx[k + 1, own]
        return carry

    lax.fori_loop(0, 8, results, 0)
    for cp in late:
        cp.wait_recv()
    for cp in early_sent:
        cp.wait_send()

    for cp in gather:
        cp.wait_recv()
    for j in range(8):
        lane = pl.ds(128 * j, 128)
        cex[0:4, lane] = ce[j]
        cex[4:8, lane] = ce[8 + j]
        cex[8:12, lane] = ch[j]
        cex[12:16, lane] = ch[8 + j]
    v = cex[...]
    w = v + fp[2]
    ex[0] = (v - tx[...]) * inv[...]
    ex[1] = w
    ex[2, own] = dec * mid(w) + fp[1, own]

    def finish(b, carry):
        e = ex[b]
        a1 = ap(e)
        a2 = ap(a1)
        a3 = mid(ap(a2))
        e, a1, a2 = mid(e), mid(a1), mid(a2)
        k = 8 * b
        ob[k] += e + a1
        ob[k + 1] += e + 2.0 * a1
        ob[k + 2] += e + 3.0 * a1 + 2.0 * a2
        ob[k + 3] += e + 4.0 * a1
        ob[k + 4] += e + 5.0 * a1 + 4.0 * a2
        ob[k + 5] += e + 6.0 * a1 + 8.0 * a2
        ob[k + 6] += e + 7.0 * a1 + 14.0 * a2 + 8.0 * a3
        ob[k + 7] += ex[b + 1, own]
        return carry

    lax.fori_loop(0, 2, finish, 0)
    for cp in gather:
        cp.total.wait_send()


def body(slabs, strips, u_coarse_guess, forcing, u_init, diffuse, vel_x, vel_y, react):
    points, rows, cols = u_coarse_guess.shape
    wide = rows + 2 * PAD
    around = rows + 2 * NEAR
    copies = 4 + 4 + 3 + 3 + 2 + 10 + 3 + 2 + 3 + 1 + 2 + 2
    f32 = jnp.float32

    def vmem(*shape):
        return pltpu.VMEM(shape, f32)

    return pl.pallas_call(
        functools.partial(kernel, slabs, strips),
        out_shape=pltpu.VMEM(forcing.shape, f32),
        in_specs=[pl.BlockSpec(memory_space=pltpu.HBM)] * 7,
        out_specs=pl.BlockSpec(memory_space=pltpu.VMEM),
        scratch_shapes=[
            vmem(points + 1, around, cols),
            vmem(points, around, cols),
            vmem(points, rows, cols),
            vmem(4, rows, cols),
            vmem(4, rows, cols),
            vmem(4, rows, cols),
            vmem(5, wide, cols),
            vmem(5, around, cols),
            vmem(around, cols),
            vmem(3, around, cols),
            vmem(wide, cols),
            vmem(3, DEPTH + 1, rows, cols),
            vmem(points + 1, around, cols),
            vmem(points + 1, around, cols),
            vmem(3, wide, cols),
            vmem(2, 3, rows, cols),
            vmem(3, around, cols),
            vmem(around, cols),
            vmem(3, around, cols),
            vmem(rows, cols),
            vmem(rows, cols),
            vmem(rows, cols),
            vmem(3, GROUP, 4, 128),
            vmem(GROUP, 4, 128),
            vmem(3, GROUP, 4, 128),
            vmem(GROUP, 4, 128),
            vmem(GROUP, 4, 128),
            vmem(slabs, 4, 128),
            vmem(GROUP, 4, 128),
            vmem(GROUP, 4, 128),
            vmem(GROUP, 4, 128),
            vmem(around, cols),
            pltpu.SemaphoreType.DMA((8,)),
            pltpu.SemaphoreType.DMA((copies,)),
            pltpu.SemaphoreType.DMA((copies,)),
        ],
        compiler_params=pltpu.CompilerParams(
            collective_id=0, has_side_effects=True, vmem_limit_bytes=60 << 20
        ),
        cost_estimate=pl.CostEstimate(flops=10_000_000, bytes_accessed=1_500_000, transcendentals=16384),
    )(
        u_coarse_guess,
        forcing.reshape(points, 2, rows, cols),
        u_init,
        diffuse,
        vel_x,
        vel_y,
        react,
    )


def solution(mesh):
    slabs = mesh.shape["tm"] // GROUP
    strips = mesh.shape["space"]
    whole = P("tm", "space", None)
    row = P("space", None)
    return jax.shard_map(
        functools.partial(body, slabs, strips),
        mesh=mesh,
        in_specs=(whole, whole) + (row,) * 5,
        out_specs=whole,
        check_vma=False,
    )
```

```python
import functools

import jax
import jax.numpy as jnp
from jax import lax
from jax.experimental import pallas as pl
from jax.experimental.pallas import tpu as pltpu
from jax.sharding import PartitionSpec as P

MESH = pl.DeviceIdType.MESH
GROUP = 16
PAD = 8
NEAR = 4
DEPTH = 6


def add_squares(x):
    out = []
    for m in range(len(x) + 2):
        terms = []
        if m < len(x):
            terms.append(x[m])
        if 1 <= m <= len(x):
            terms.append(2.0 * x[m - 1])
        if 2 <= m <= len(x) + 1:
            terms.append(x[m - 2])
        total = terms[0]
        for t in terms[1:]:
            total = total + t
        out.append(total)
    return out


def kernel(
    slabs,
    strips,
    guess,
    force,
    init,
    diffuse,
    vel_x,
    vel_y,
    react,
    ob,
    gx,
    fx,
    hx,
    cx,
    cn,
    cf,
    wx,
    wn,
    inv,
    rn,
    decx,
    px,
    dx,
    zx,
    rx,
    qx,
    fp,
    tx,
    ex,
    ini,
    g7,
    d7,
    sp,
    dp,
    r1,
    pre,
    pw,
    r2,
    wo,
    ce,
    ch,
    cex,
    lsem,
    ss,
    sr,
    known,
):
    tm = lax.axis_index("tm")
    sx = lax.axis_index("space")
    y = tm // GROUP
    q = lax.rem(tm, GROUP)
    count = slabs * GROUP
    xs = (lax.rem(sx + 1, strips), lax.rem(sx + strips - 1, strips))
    nxt = lax.rem(tm + 1, count)
    prv = lax.rem(tm + count - 1, count)
    last = tm == count - 1
    cols = ob.shape[2]
    own = pl.ds(0, 8)
    centre_rows = pl.ds(PAD, 8)

    zc = q // 2
    core = lax.rem(q, 2)
    depth = GROUP // 2

    def along_z(m, c):
        return y * GROUP + lax.rem(zc + m + depth, depth) * 2 + c

    def along_y(m):
        return lax.rem(y + m + slabs, slabs) * GROUP + q

    barrier = pltpu.get_barrier_semaphore()
    peers = [(tm, s) for s in xs] + [(nxt, sx), (prv, sx)]
    for s in (sx,) + xs:
        peers.append((along_z(0, 1 - core), s))
        for m in (-2, -1, 1, 2):
            peers += [(along_z(m, 0), s), (along_z(m, 1), s)]
    for m in (-2, -1, 1, 2):
        peers.append((along_y(m), sx))
    for dev in peers:
        pl.semaphore_signal(barrier, inc=1, device_id=dev, device_id_type=MESH)

    loads = []
    for i, (src, dst) in enumerate(
        [
            (guess, gx.at[pl.ds(1, 8), own]),
            (force.at[:, 0], fx.at[:, own]),
            (force.at[:, 1], hx),
            (init, ini),
            (diffuse, cx.at[0]),
            (vel_x, cx.at[1]),
            (vel_y, cx.at[2]),
            (react, cx.at[3]),
        ]
    ):
        cp = pltpu.make_async_copy(src, dst, lsem.at[i])
        cp.start()
        loads.append(cp)
    for cp in loads:
        cp.wait()

    sent = []
    slot = [0]

    def send(src, dst, dev):
        i = slot[0]
        slot[0] += 1
        cp = pltpu.make_async_remote_copy(
            src_ref=src,
            dst_ref=dst,
            send_sem=ss.at[i],
            recv_sem=sr.at[i],
            device_id=dev,
            device_id_type=MESH,
        )
        cp.start()
        sent.append(cp)
        return cp

    class Batch:
        def __init__(self, items, whole):
            i = slot[0]
            slot[0] += 1
            for src, dst, dev in items:
                self.copy = pltpu.make_async_remote_copy(
                    src_ref=src,
                    dst_ref=dst,
                    send_sem=ss.at[i],
                    recv_sem=sr.at[i],
                    device_id=dev,
                    device_id_type=MESH,
                )
                self.copy.start()
            self.total = pltpu.make_async_remote_copy(
                src_ref=whole,
                dst_ref=whole,
                send_sem=ss.at[i],
                recv_sem=sr.at[i],
                device_id=items[0][2],
                device_id_type=MESH,
            )
            sent.append(self.total)

        def wait_recv(self):
            self.total.wait_recv()

    def far_first(n):
        return sorted(range(1, n), key=lambda m: -min(m, n - m))

    def halo(ref, lead, h):
        a = send(ref.at[lead + (pl.ds(8 - h, h),)], ref.at[lead + (pl.ds(16 - h, h),)], (tm, xs[0]))
        b = send(ref.at[lead + (pl.ds(0, h),)], ref.at[lead + (pl.ds(8, h),)], (tm, xs[1]))
        return [a, b]

    def onward(src, ref, lead, h):
        return [
            send(src, ref.at[lead + (own,)], (nxt, sx)),
            send(src.at[pl.ds(8 - h, h)], ref.at[lead + (pl.ds(16 - h, h),)], (nxt, xs[0])),
            send(src.at[pl.ds(0, h)], ref.at[lead + (pl.ds(8, h),)], (nxt, xs[1])),
        ]

    def change(G, F, H, k):
        return (G[k - 1] + F[k] + H[k] - G[k], 2.0 * G[k - 1] + F[k], G[k - 1])

    def reader(ref, lane, shift, padded):
        def read(k):
            if padded:
                return ref[k + shift, own, lane]
            return ref[k + shift, :, lane]

        class Reader:
            def __getitem__(self, k):
                return read(k)

        return Reader()

    def fields(lane):
        return reader(gx, lane, 1, True), reader(fx, lane, 0, True), reader(hx, lane, 0, False)

    def first(lane):
        G, F, H = fields(lane)
        d0, d1, d2 = [jnp.where(last, 0.0, v) for v in change(G, F, H, 7)]
        g = jnp.where(last, ini[:, lane], G[7])
        g7[:, lane] = g
        return [
            d0 + g,
            d1 + 6.0 * (d0 + g),
            d2 + 6.0 * d1 + 8.0 * d0 + 9.0 * g,
            6.0 * d2 + 8.0 * d1 + 4.0 * g,
            8.0 * d2,
        ]

    def second(lane):
        G, F, H = fields(lane)
        a0, a1, a2 = change(G, F, H, 3)
        b0, b1, b2 = change(G, F, H, 4)
        c0, c1, c2 = change(G, F, H, 5)
        e0, e1, e2 = change(G, F, H, 6)
        return [
            a0 + b0 + c0 + e0,
            a1 + 6.0 * a0 + b1 + 4.0 * b0 + c1 + 2.0 * c0 + e1,
            a2 + 6.0 * a1 + 8.0 * a0 + b2 + 4.0 * b1 + c2 + 2.0 * c1 + e2,
            6.0 * a2 + 8.0 * a1 + 4.0 * b2 + 2.0 * c2,
            8.0 * a2,
        ]

    def third(lane):
        G, F, H = fields(lane)
        b1 = F[0]
        b0 = b1 + H[0] - G[0]
        c0, c1, c2 = change(G, F, H, 1)
        e0, e1, e2 = change(G, F, H, 2)
        return [
            b0 + c0 + e0,
            b1 + 4.0 * b0 + c1 + 2.0 * c0 + e1,
            4.0 * b1 + c2 + 2.0 * c1 + e2,
            2.0 * c2,
        ]

    def combine(p, make):
        def one(j, carry):
            lane = pl.ds(pl.multiple_of(j * 128, 128), 128)
            for m, v in enumerate(add_squares(make(lane))):
                px[p, m, :, lane] = v
            return carry

        lax.fori_loop(0, cols // 128, one, 0)

    pl.semaphore_wait(barrier, len(peers))
    word = [along_z(-2, core), along_z(2, core), along_y(-2), along_y(2), prv]
    for dev in word:
        pl.semaphore_signal(known, inc=1, device_id=(dev, sx), device_id_type=MESH)

    def parameters(dst, up, down, n):
        return [
            send(cx.at[:, pl.ds(up, n)], dst.at[:, pl.ds(up, n)], (tm, xs[0])),
            send(cx.at[:, pl.ds(down, n)], dst.at[:, pl.ds(down, n)], (tm, xs[1])),
        ]

    near = parameters(cn, 8 - NEAR, 0, NEAR)
    far = parameters(cf, 8 - DEPTH, NEAR, DEPTH - NEAR)
    early = halo(gx, (pl.ds(1, 7),), 2) + halo(fx, (slice(None),), 1)
    combine(0, first)
    combine(1, second)
    combine(2, third)

    row = lax.broadcasted_iota(jnp.int32, (8, cols), 0)
    col = lax.broadcasted_iota(jnp.int32, (8, cols), 1)
    low = row < NEAR
    above = sx > 0
    beneath = sx < strips - 1

    def weights(raw, inside, top, bottom):
        dif, vx, vy, rea = raw
        west = jnp.where(col == 0, 0.0, dif + jnp.maximum(vx, 0.0))
        east = jnp.where(col == cols - 1, 0.0, dif - jnp.minimum(vx, 0.0))
        north = dif + jnp.maximum(vy, 0.0)
        south = dif - jnp.minimum(vy, 0.0)
        centre = -(4.0 * dif + jnp.abs(vx) + jnp.abs(vy) + rea)
        if inside is not None:
            return [jnp.where(inside, v, 0.0) for v in (west, east, north, south, centre)]
        return [west, east, jnp.where(top, 0.0, north), jnp.where(bottom, 0.0, south), centre]

    raw = [cx[i] for i in range(4)]
    edge = weights(raw, None, (row == 0) & (sx == 0), (row == 7) & (sx == strips - 1))
    for i, v in enumerate(edge):
        wx[i, 8:16] = v
        wn[i, 0:8] = v
    decx[8:16] = jnp.exp(-8.0 * raw[3])
    inv[0:8] = jnp.exp(8.0 * raw[3])

    pl.semaphore_wait(known, len(word))
    early += onward(g7, gx, (0,), 2)
    for cp in near:
        cp.wait_recv()
    raw = [cn[i] for i in range(4)]
    for i, v in enumerate(weights(raw, (low & beneath) | (~low & above), None, None)):
        wn[i, 8:16] = v
    inv[8:16] = jnp.exp(8.0 * raw[3])

    def stencil(w, v):
        n = v.shape[0]
        return (
            w[4] * v
            + w[0] * pltpu.roll(v, 1, 1)
            + w[1] * pltpu.roll(v, cols - 1, 1)
            + w[2] * pltpu.roll(v, 1, 0)
            + w[3] * pltpu.roll(v, n - 1, 0)
        )

    def ap(v):
        return stencil(wn, v)

    def mid(v):
        return v[0:8]

    def around(v):
        none = jnp.zeros_like(v)
        return jnp.concatenate([none, v, none], axis=0)

    def horner_near(p, carry):
        top = DEPTH - p // 2

        def start(m):
            v = px[p, m]
            return jnp.concatenate([v, jnp.zeros_like(v)], axis=0)

        def level(i, v):
            return ap(v) + start(top - 1 - i)

        rn[p] = lax.fori_loop(0, NEAR, level, start(top))
        return carry

    lax.fori_loop(0, 3, horner_near, 0)

    for cp in far:
        cp.wait_recv()
    for t, inside in ((0, (row >= PAD - DEPTH) & above), (2, (row < DEPTH) & beneath)):
        raw = [jnp.where(low, cn[i] if t else cf[i], cf[i] if t else cn[i]) for i in range(4)]
        for i, v in enumerate(weights(raw, inside, None, None)):
            wx[i, 8 * t : 8 * t + 8] = v
        decx[8 * t : 8 * t + 8] = jnp.where(inside, jnp.exp(-8.0 * raw[3]), 0.0)

    def horner_far(p, carry):
        top = DEPTH - p // 2

        def level(i, v):
            return stencil(wx, v) + around(px[p, top - 1 - NEAR - i])

        v = rn[p, 8:16]
        v = jnp.concatenate([jnp.where(low, 0.0, v), rn[p, 0:8], jnp.where(low, v, 0.0)], axis=0)
        rx[p] = lax.fori_loop(0, top - NEAR, level, v)
        return carry

    lax.fori_loop(0, 3, horner_far, 0)

    decv = decx[...]
    dec = decv[8:16]
    value = rx[0]
    part = jnp.where(last, value, decv * (decv * rx[2] + rx[1]) + value)
    for h in (0, 1):
        for j in range(8):
            dp[8 * h + j] = dec[4 * h : 4 * h + 4, 128 * j : 128 * j + 128]
            for t in range(3):
                r = 8 * t + 4 * h
                sp[t, 8 * h + j] = part[r : r + 4, 128 * j : 128 * j + 128]

    def mate(m):
        to = lax.rem(q + m, GROUP)
        return to, y * GROUP + to

    items = ([], [], [])
    for m in far_first(GROUP) + [0]:
        to, dev = mate(m)
        items[2].append((sp.at[2, to], r1.at[2, q], (dev, xs[0])))
        items[0].append((sp.at[0, to], r1.at[0, q], (dev, xs[1])))
        if m:
            items[1].append((sp.at[1, to], r1.at[1, q], (dev, sx)))
    scatter = [Batch(items[2], r1.at[2]), Batch(items[0], r1.at[0]), Batch(items[1], r1.at[1, pl.ds(0, GROUP - 1)])]
    r1[1, q] = sp[1, q]
    spill = [
        send(rx.at[:, pl.ds(16, DEPTH)], qx.at[0, :, pl.ds(0, DEPTH)], (tm, xs[0])),
        send(rx.at[:, pl.ds(8 - DEPTH, DEPTH)], qx.at[1, :, pl.ds(8 - DEPTH, DEPTH)], (tm, xs[1])),
    ]
    d1 = dp[q]
    d2 = d1 * d1

    for cp in early:
        cp.wait_recv()

    def changes(k, carry):
        g, f = gx[k], fx[k]
        v = ap(g) + 2.0 * g + f
        dx[k + 1, own] = mid(ap(v)) + mid(g + f) + hx[k] - gx[k + 1, own]
        return carry

    lax.fori_loop(0, 8, changes, 0)
    d7[...] = jnp.where(last, 0.0, dx[8, own])
    middle = []
    for k, h in ((0, 3), (1, 2), (3, 4), (4, 3), (5, 2)):
        middle += halo(dx, (k + 1,), h)
    middle += onward(d7, dx, (0,), 4)
    for cp in spill:
        cp.wait_recv()
    for p in range(3):
        over = jnp.where(row < DEPTH, qx[0, p], 0.0)
        under = jnp.where(row >= 8 - DEPTH, qx[1, p], 0.0)
        fp[p, own] = rx[p, centre_rows] + over + under
    late = halo(fp, (2,), 3) + onward(fp.at[0, own], tx, (), 3)

    for cp in scatter:
        cp.wait_recv()
    acc = jnp.zeros_like(d2)
    fac = jnp.ones_like(d2)
    for i in range(GROUP):
        pre[i] = acc
        pw[i] = fac
        part = r1[1, i] + r1[2, i] + r1[0, i]
        acc = d2 * acc + part
        fac = d2 * fac
    r2[y] = jnp.where(y == slabs - 1, part, acc)
    items = []
    for m in far_first(slabs):
        items.append((r2.at[y], r2.at[y], (lax.rem(y + m, slabs) * GROUP + q, sx)))
    across = [Batch(items, r2.at[pl.ds(0, slabs - 1)])]

    for cp in middle:
        cp.wait_recv()
    zx[0] = gx[0] + dx[0]

    def twice(v):
        v = v + ap(v)
        return mid(v) + mid(ap(v))

    def blocks(b, carry):
        k = 4 * b
        a = dx[k]
        bb = dx[k + 1]
        c = dx[k + 2]
        zx[k + 1, own] = gx[k + 1, own] + mid(bb) + twice(a)
        w = a + 2.0 * ap(a) + bb
        zx[k + 2, own] = gx[k + 2, own] + mid(c) + twice(w)
        w = w + 2.0 * ap(w) + c
        zx[k + 3, own] = gx[k + 3, own] + dx[k + 3, own] + twice(w)
        zx[k + 4, own] = gx[k + 4, own] + dx[k + 4, own]
        return carry

    lax.fori_loop(0, 2, blocks, 0)
    coarse = halo(zx, (pl.ds(1, 7),), 1)

    for cp in across:
        cp.wait_recv()
    acc = r2[slabs - 1]
    for i in range(slabs - 1):
        acc = jnp.where(i < y, fac * acc + r2[i], acc)
    for i in range(GROUP):
        wo[i] = pw[i] * acc + pre[i]
    half = q // 8
    side = lax.rem(sx + 2 * half + strips - 1, strips)
    items = ([], [])
    for m in far_first(GROUP) + [0]:
        to, dev = mate(m)
        items[0].append((wo.at[to], ch.at[q], (dev, side)))
        if m:
            items[1].append((wo.at[to], ce.at[q], (dev, sx)))
    early_sent = list(sent)
    gather = [Batch(items[0], ch), Batch(items[1], ce.at[pl.ds(0, GROUP - 1)])]
    ce[q] = wo[q]

    for cp in coarse:
        cp.wait_recv()

    def results(k, carry):
        v = zx[k]
        ob[2 * k] = mid(v) + mid(ap(v)) + fx[k, own]
        ob[2 * k + 1] = zx[k + 1, own]
        return carry

    lax.fori_loop(0, 8, results, 0)
    for cp in late:
        cp.wait_recv()
    for cp in early_sent:
        cp.wait_send()

    for cp in gather:
        cp.wait_recv()
    for j in range(8):
        lane = pl.ds(128 * j, 128)
        cex[0:4, lane] = ce[j]
        cex[4:8, lane] = ce[8 + j]
        cex[8:12, lane] = ch[j]
        cex[12:16, lane] = ch[8 + j]
    v = cex[...]
    w = v + fp[2]
    ex[0] = (v - tx[...]) * inv[...]
    ex[1] = w
    ex[2, own] = dec * mid(w) + fp[1, own]

    def finish(b, carry):
        e = ex[b]
        a1 = ap(e)
        a2 = ap(a1)
        a3 = mid(ap(a2))
        e, a1, a2 = mid(e), mid(a1), mid(a2)
        k = 8 * b
        ob[k] += e + a1
        ob[k + 1] += e + 2.0 * a1
        ob[k + 2] += e + 3.0 * a1 + 2.0 * a2
        ob[k + 3] += e + 4.0 * a1
        ob[k + 4] += e + 5.0 * a1 + 4.0 * a2
        ob[k + 5] += e + 6.0 * a1 + 8.0 * a2
        ob[k + 6] += e + 7.0 * a1 + 14.0 * a2 + 8.0 * a3
        ob[k + 7] += ex[b + 1, own]
        return carry

    lax.fori_loop(0, 2, finish, 0)
    for cp in gather:
        cp.total.wait_send()


def body(slabs, strips, u_coarse_guess, forcing, u_init, diffuse, vel_x, vel_y, react):
    points, rows, cols = u_coarse_guess.shape
    wide = rows + 2 * PAD
    around = rows + 2 * NEAR
    copies = 4 + 4 + 3 + 3 + 2 + 10 + 3 + 2 + 3 + 1 + 2 + 2
    f32 = jnp.float32

    def vmem(*shape):
        return pltpu.VMEM(shape, f32)

    return pl.pallas_call(
        functools.partial(kernel, slabs, strips),
        out_shape=pltpu.VMEM(forcing.shape, f32),
        in_specs=[pl.BlockSpec(memory_space=pltpu.HBM)] * 7,
        out_specs=pl.BlockSpec(memory_space=pltpu.VMEM),
        scratch_shapes=[
            vmem(points + 1, around, cols),
            vmem(points, around, cols),
            vmem(points, rows, cols),
            vmem(4, rows, cols),
            vmem(4, rows, cols),
            vmem(4, rows, cols),
            vmem(5, wide, cols),
            vmem(5, around, cols),
            vmem(around, cols),
            vmem(3, around, cols),
            vmem(wide, cols),
            vmem(3, DEPTH + 1, rows, cols),
            vmem(points + 1, around, cols),
            vmem(points + 1, around, cols),
            vmem(3, wide, cols),
            vmem(2, 3, rows, cols),
            vmem(3, around, cols),
            vmem(around, cols),
            vmem(3, around, cols),
            vmem(rows, cols),
            vmem(rows, cols),
            vmem(rows, cols),
            vmem(3, GROUP, 4, 128),
            vmem(GROUP, 4, 128),
            vmem(3, GROUP, 4, 128),
            vmem(GROUP, 4, 128),
            vmem(GROUP, 4, 128),
            vmem(slabs, 4, 128),
            vmem(GROUP, 4, 128),
            vmem(GROUP, 4, 128),
            vmem(GROUP, 4, 128),
            vmem(around, cols),
            pltpu.SemaphoreType.DMA((8,)),
            pltpu.SemaphoreType.DMA((copies,)),
            pltpu.SemaphoreType.DMA((copies,)),
            pltpu.SemaphoreType.REGULAR,
        ],
        compiler_params=pltpu.CompilerParams(
            collective_id=0, has_side_effects=True, vmem_limit_bytes=60 << 20
        ),
        cost_estimate=pl.CostEstimate(flops=10_000_000, bytes_accessed=1_500_000, transcendentals=16384),
    )(
        u_coarse_guess,
        forcing.reshape(points, 2, rows, cols),
        u_init,
        diffuse,
        vel_x,
        vel_y,
        react,
    )


def solution(mesh):
    slabs = mesh.shape["tm"] // GROUP
    strips = mesh.shape["space"]
    whole = P("tm", "space", None)
    row = P("space", None)
    return jax.shard_map(
        functools.partial(body, slabs, strips),
        mesh=mesh,
        in_specs=(whole, whole) + (row,) * 5,
        out_specs=whole,
        check_vma=False,
    )
```

```python
import functools

import jax
import jax.numpy as jnp
from jax import lax
from jax.experimental import pallas as pl
from jax.experimental.pallas import tpu as pltpu
from jax.sharding import PartitionSpec as P

MESH = pl.DeviceIdType.MESH
GROUP = 16
PAD = 8
NEAR = 4
DEPTH = 6


def add_squares(x):
    out = []
    for m in range(len(x) + 2):
        terms = []
        if m < len(x):
            terms.append(x[m])
        if 1 <= m <= len(x):
            terms.append(2.0 * x[m - 1])
        if 2 <= m <= len(x) + 1:
            terms.append(x[m - 2])
        total = terms[0]
        for t in terms[1:]:
            total = total + t
        out.append(total)
    return out


def kernel(
    slabs,
    strips,
    guess,
    force,
    init,
    diffuse,
    vel_x,
    vel_y,
    react,
    ob,
    gx,
    fx,
    hx,
    cx,
    cn,
    cf,
    wx,
    wn,
    inv,
    rn,
    decx,
    px,
    dx,
    zx,
    rx,
    qx,
    fp,
    tx,
    ini,
    g7,
    d7,
    sp,
    dp,
    r1,
    pre,
    pw,
    r2,
    wo,
    ce,
    ch,
    cex,
    lsem,
    ss,
    sr,
    known,
):
    tm = lax.axis_index("tm")
    sx = lax.axis_index("space")
    y = tm // GROUP
    q = lax.rem(tm, GROUP)
    count = slabs * GROUP
    xs = (lax.rem(sx + 1, strips), lax.rem(sx + strips - 1, strips))
    nxt = lax.rem(tm + 1, count)
    prv = lax.rem(tm + count - 1, count)
    last = tm == count - 1
    cols = ob.shape[2]
    own = pl.ds(0, 8)
    centre_rows = pl.ds(PAD, 8)

    zc = q // 2
    core = lax.rem(q, 2)
    depth = GROUP // 2

    def along_z(m, c):
        return y * GROUP + lax.rem(zc + m + depth, depth) * 2 + c

    def along_y(m):
        return lax.rem(y + m + slabs, slabs) * GROUP + q

    barrier = pltpu.get_barrier_semaphore()
    peers = [(tm, s) for s in xs] + [(nxt, sx), (prv, sx)]
    for s in (sx,) + xs:
        peers.append((along_z(0, 1 - core), s))
        for m in (-2, -1, 1, 2):
            peers += [(along_z(m, 0), s), (along_z(m, 1), s)]
    for m in (-2, -1, 1, 2):
        peers.append((along_y(m), sx))
    for dev in peers:
        pl.semaphore_signal(barrier, inc=1, device_id=dev, device_id_type=MESH)

    loads = []
    for i, (src, dst) in enumerate(
        [
            (guess, gx.at[pl.ds(1, 8), own]),
            (force.at[:, 0], fx.at[:, own]),
            (force.at[:, 1], hx),
            (init, ini),
            (diffuse, cx.at[0]),
            (vel_x, cx.at[1]),
            (vel_y, cx.at[2]),
            (react, cx.at[3]),
        ]
    ):
        cp = pltpu.make_async_copy(src, dst, lsem.at[i])
        cp.start()
        loads.append(cp)
    for cp in loads:
        cp.wait()

    sent = []
    slot = [0]

    def send(src, dst, dev):
        i = slot[0]
        slot[0] += 1
        cp = pltpu.make_async_remote_copy(
            src_ref=src,
            dst_ref=dst,
            send_sem=ss.at[i],
            recv_sem=sr.at[i],
            device_id=dev,
            device_id_type=MESH,
        )
        cp.start()
        sent.append(cp)
        return cp

    class Batch:
        def __init__(self, items, whole):
            i = slot[0]
            slot[0] += 1
            for src, dst, dev in items:
                self.copy = pltpu.make_async_remote_copy(
                    src_ref=src,
                    dst_ref=dst,
                    send_sem=ss.at[i],
                    recv_sem=sr.at[i],
                    device_id=dev,
                    device_id_type=MESH,
                )
                self.copy.start()
            self.total = pltpu.make_async_remote_copy(
                src_ref=whole,
                dst_ref=whole,
                send_sem=ss.at[i],
                recv_sem=sr.at[i],
                device_id=items[0][2],
                device_id_type=MESH,
            )
            sent.append(self.total)

        def wait_recv(self):
            self.total.wait_recv()

    def far_first(n):
        return sorted(range(1, n), key=lambda m: -min(m, n - m))

    def halo(ref, lead, h):
        a = send(ref.at[lead + (pl.ds(8 - h, h),)], ref.at[lead + (pl.ds(16 - h, h),)], (tm, xs[0]))
        b = send(ref.at[lead + (pl.ds(0, h),)], ref.at[lead + (pl.ds(8, h),)], (tm, xs[1]))
        return [a, b]

    def onward(src, ref, lead, h):
        return [
            send(src, ref.at[lead + (own,)], (nxt, sx)),
            send(src.at[pl.ds(8 - h, h)], ref.at[lead + (pl.ds(16 - h, h),)], (nxt, xs[0])),
            send(src.at[pl.ds(0, h)], ref.at[lead + (pl.ds(8, h),)], (nxt, xs[1])),
        ]

    def change(G, F, H, k):
        return (G[k - 1] + F[k] + H[k] - G[k], 2.0 * G[k - 1] + F[k], G[k - 1])

    def reader(ref, lane, shift, padded):
        def read(k):
            if padded:
                return ref[k + shift, own, lane]
            return ref[k + shift, :, lane]

        class Reader:
            def __getitem__(self, k):
                return read(k)

        return Reader()

    def fields(lane):
        return reader(gx, lane, 1, True), reader(fx, lane, 0, True), reader(hx, lane, 0, False)

    def first(lane):
        G, F, H = fields(lane)
        d0, d1, d2 = [jnp.where(last, 0.0, v) for v in change(G, F, H, 7)]
        g = jnp.where(last, ini[:, lane], G[7])
        g7[:, lane] = g
        return [
            d0 + g,
            d1 + 6.0 * (d0 + g),
            d2 + 6.0 * d1 + 8.0 * d0 + 9.0 * g,
            6.0 * d2 + 8.0 * d1 + 4.0 * g,
            8.0 * d2,
        ]

    def second(lane):
        G, F, H = fields(lane)
        a0, a1, a2 = change(G, F, H, 3)
        b0, b1, b2 = change(G, F, H, 4)
        c0, c1, c2 = change(G, F, H, 5)
        e0, e1, e2 = change(G, F, H, 6)
        return [
            a0 + b0 + c0 + e0,
            a1 + 6.0 * a0 + b1 + 4.0 * b0 + c1 + 2.0 * c0 + e1,
            a2 + 6.0 * a1 + 8.0 * a0 + b2 + 4.0 * b1 + c2 + 2.0 * c1 + e2,
            6.0 * a2 + 8.0 * a1 + 4.0 * b2 + 2.0 * c2,
            8.0 * a2,
        ]

    def third(lane):
        G, F, H = fields(lane)
        b1 = F[0]
        b0 = b1 + H[0] - G[0]
        c0, c1, c2 = change(G, F, H, 1)
        e0, e1, e2 = change(G, F, H, 2)
        return [
            b0 + c0 + e0,
            b1 + 4.0 * b0 + c1 + 2.0 * c0 + e1,
            4.0 * b1 + c2 + 2.0 * c1 + e2,
            2.0 * c2,
        ]

    def combine(p, make):
        def one(j, carry):
            lane = pl.ds(pl.multiple_of(j * 128, 128), 128)
            for m, v in enumerate(add_squares(make(lane))):
                px[p, m, :, lane] = v
            return carry

        lax.fori_loop(0, cols // 128, one, 0)

    pl.semaphore_wait(barrier, len(peers))
    word = [along_z(-2, core), along_z(2, core), along_y(-2), along_y(2), prv]
    for dev in word:
        pl.semaphore_signal(known, inc=1, device_id=(dev, sx), device_id_type=MESH)

    def parameters(dst, up, down, n):
        return [
            send(cx.at[:, pl.ds(up, n)], dst.at[:, pl.ds(up, n)], (tm, xs[0])),
            send(cx.at[:, pl.ds(down, n)], dst.at[:, pl.ds(down, n)], (tm, xs[1])),
        ]

    near = parameters(cn, 8 - NEAR, 0, NEAR)
    far = parameters(cf, 8 - DEPTH, NEAR, DEPTH - NEAR)
    early = halo(gx, (pl.ds(1, 7),), 2) + halo(fx, (slice(None),), 1)
    combine(0, first)
    combine(1, second)
    combine(2, third)

    row = lax.broadcasted_iota(jnp.int32, (8, cols), 0)
    col = lax.broadcasted_iota(jnp.int32, (8, cols), 1)
    low = row < NEAR
    above = sx > 0
    beneath = sx < strips - 1

    def weights(raw, inside, top, bottom):
        dif, vx, vy, rea = raw
        west = jnp.where(col == 0, 0.0, dif + jnp.maximum(vx, 0.0))
        east = jnp.where(col == cols - 1, 0.0, dif - jnp.minimum(vx, 0.0))
        north = dif + jnp.maximum(vy, 0.0)
        south = dif - jnp.minimum(vy, 0.0)
        centre = -(4.0 * dif + jnp.abs(vx) + jnp.abs(vy) + rea)
        if inside is not None:
            return [jnp.where(inside, v, 0.0) for v in (west, east, north, south, centre)]
        return [west, east, jnp.where(top, 0.0, north), jnp.where(bottom, 0.0, south), centre]

    raw = [cx[i] for i in range(4)]
    edge = weights(raw, None, (row == 0) & (sx == 0), (row == 7) & (sx == strips - 1))
    for i, v in enumerate(edge):
        wx[i, 8:16] = v
        wn[i, 0:8] = v
    decx[8:16] = jnp.exp(-8.0 * raw[3])
    inv[0:8] = jnp.exp(8.0 * raw[3])

    pl.semaphore_wait(known, len(word))
    early += onward(g7, gx, (0,), 2)
    for cp in near:
        cp.wait_recv()
    raw = [cn[i] for i in range(4)]
    for i, v in enumerate(weights(raw, (low & beneath) | (~low & above), None, None)):
        wn[i, 8:16] = v
    inv[8:16] = jnp.exp(8.0 * raw[3])

    def stencils(w, values):
        n = values[0].shape[0]
        total = [w[4] * v for v in values]
        for i, shift, axis in ((0, 1, 1), (1, cols - 1, 1), (2, 1, 0), (3, n - 1, 0)):
            weight = w[i]
            total = [t + weight * pltpu.roll(v, shift, axis) for t, v in zip(total, values)]
        return total

    def stencil(w, v):
        return stencils(w, [v])[0]

    def ap(v):
        return stencil(wn, v)

    def mid(v):
        return v[0:8]

    def around(v):
        none = jnp.zeros_like(v)
        return jnp.concatenate([none, v, none], axis=0)

    tops = (DEPTH, DEPTH, DEPTH - 1)

    def start(p, m):
        v = px[p, m]
        return jnp.concatenate([v, jnp.zeros_like(v)], axis=0)

    for p in range(3):
        rn[p] = start(p, tops[p])

    def level_near(i, carry):
        new = stencils(wn, [rn[p] for p in range(3)])
        for p in range(3):
            rn[p] = new[p] + start(p, tops[p] - 1 - i)
        return carry

    lax.fori_loop(0, NEAR, level_near, 0)

    for cp in far:
        cp.wait_recv()
    for t, inside in ((0, (row >= PAD - DEPTH) & above), (2, (row < DEPTH) & beneath)):
        raw = [jnp.where(low, cn[i] if t else cf[i], cf[i] if t else cn[i]) for i in range(4)]
        for i, v in enumerate(weights(raw, inside, None, None)):
            wx[i, 8 * t : 8 * t + 8] = v
        decx[8 * t : 8 * t + 8] = jnp.where(inside, jnp.exp(-8.0 * raw[3]), 0.0)

    for p in range(3):
        v = rn[p, 8:16]
        rx[p] = jnp.concatenate([jnp.where(low, 0.0, v), rn[p, 0:8], jnp.where(low, v, 0.0)], axis=0)
    for i in range(NEAR, DEPTH):
        left = [p for p in range(3) if i < tops[p]]
        new = stencils(wx, [rx[p] for p in left])
        for p in left:
            rx[p] = new[p] + around(px[p, tops[p] - 1 - i])

    decv = decx[...]
    dec = decv[8:16]
    value = rx[0]
    part = jnp.where(last, value, decv * (decv * rx[2] + rx[1]) + value)
    for h in (0, 1):
        for j in range(8):
            dp[8 * h + j] = dec[4 * h : 4 * h + 4, 128 * j : 128 * j + 128]
            for t in range(3):
                r = 8 * t + 4 * h
                sp[t, 8 * h + j] = part[r : r + 4, 128 * j : 128 * j + 128]

    def mate(m):
        to = lax.rem(q + m, GROUP)
        return to, y * GROUP + to

    items = ([], [], [])
    for m in far_first(GROUP) + [0]:
        to, dev = mate(m)
        items[2].append((sp.at[2, to], r1.at[2, q], (dev, xs[0])))
        items[0].append((sp.at[0, to], r1.at[0, q], (dev, xs[1])))
        if m:
            items[1].append((sp.at[1, to], r1.at[1, q], (dev, sx)))
    scatter = [Batch(items[2], r1.at[2]), Batch(items[0], r1.at[0]), Batch(items[1], r1.at[1, pl.ds(0, GROUP - 1)])]
    r1[1, q] = sp[1, q]
    spill = [
        send(rx.at[:, pl.ds(16, DEPTH)], qx.at[0, :, pl.ds(0, DEPTH)], (tm, xs[0])),
        send(rx.at[:, pl.ds(8 - DEPTH, DEPTH)], qx.at[1, :, pl.ds(8 - DEPTH, DEPTH)], (tm, xs[1])),
    ]
    d1 = dp[q]
    d2 = d1 * d1

    for cp in early:
        cp.wait_recv()

    def changes(k, carry):
        g, f = gx[k], fx[k]
        v = ap(g) + 2.0 * g + f
        dx[k + 1, own] = mid(ap(v)) + mid(g + f) + hx[k] - gx[k + 1, own]
        return carry

    lax.fori_loop(0, 8, changes, 0)
    d7[...] = jnp.where(last, 0.0, dx[8, own])
    middle = []
    for k, h in ((0, 3), (1, 2), (3, 4), (4, 3), (5, 2)):
        middle += halo(dx, (k + 1,), h)
    middle += onward(d7, dx, (0,), 4)
    for cp in spill:
        cp.wait_recv()
    for p in range(3):
        over = jnp.where(row < DEPTH, qx[0, p], 0.0)
        under = jnp.where(row >= 8 - DEPTH, qx[1, p], 0.0)
        fp[p, own] = rx[p, centre_rows] + over + under
    late = halo(fp, (2,), 3) + onward(fp.at[0, own], tx, (), 3)

    for cp in scatter:
        cp.wait_recv()
    acc = jnp.zeros_like(d2)
    fac = jnp.ones_like(d2)
    for i in range(GROUP):
        pre[i] = acc
        pw[i] = fac
        part = r1[1, i] + r1[2, i] + r1[0, i]
        acc = d2 * acc + part
        fac = d2 * fac
    r2[y] = jnp.where(y == slabs - 1, part, acc)
    items = []
    for m in far_first(slabs):
        items.append((r2.at[y], r2.at[y], (lax.rem(y + m, slabs) * GROUP + q, sx)))
    across = [Batch(items, r2.at[pl.ds(0, slabs - 1)])]

    for cp in middle:
        cp.wait_recv()
    zx[0] = gx[0] + dx[0]

    def twice(v):
        v = v + ap(v)
        return mid(v) + mid(ap(v))

    def blocks(b, carry):
        k = 4 * b
        a = dx[k]
        bb = dx[k + 1]
        c = dx[k + 2]
        zx[k + 1, own] = gx[k + 1, own] + mid(bb) + twice(a)
        w = a + 2.0 * ap(a) + bb
        zx[k + 2, own] = gx[k + 2, own] + mid(c) + twice(w)
        w = w + 2.0 * ap(w) + c
        zx[k + 3, own] = gx[k + 3, own] + dx[k + 3, own] + twice(w)
        zx[k + 4, own] = gx[k + 4, own] + dx[k + 4, own]
        return carry

    lax.fori_loop(0, 2, blocks, 0)
    coarse = halo(zx, (pl.ds(1, 7),), 1)

    for cp in across:
        cp.wait_recv()
    acc = r2[slabs - 1]
    for i in range(slabs - 1):
        acc = jnp.where(i < y, fac * acc + r2[i], acc)
    for i in range(GROUP):
        wo[i] = pw[i] * acc + pre[i]
    half = q // 8
    side = lax.rem(sx + 2 * half + strips - 1, strips)
    items = ([], [])
    for m in far_first(GROUP) + [0]:
        to, dev = mate(m)
        items[0].append((wo.at[to], ch.at[q], (dev, side)))
        if m:
            items[1].append((wo.at[to], ce.at[q], (dev, sx)))
    early_sent = list(sent)
    gather = [Batch(items[0], ch), Batch(items[1], ce.at[pl.ds(0, GROUP - 1)])]
    ce[q] = wo[q]

    for cp in coarse:
        cp.wait_recv()

    def results(k, carry):
        v = zx[k]
        ob[2 * k] = mid(v) + mid(ap(v)) + fx[k, own]
        ob[2 * k + 1] = zx[k + 1, own]
        return carry

    lax.fori_loop(0, 8, results, 0)
    for cp in late:
        cp.wait_recv()
    for cp in early_sent:
        cp.wait_send()

    for cp in gather:
        cp.wait_recv()
    for j in range(8):
        lane = pl.ds(128 * j, 128)
        cex[0:4, lane] = ce[j]
        cex[4:8, lane] = ce[8 + j]
        cex[8:12, lane] = ch[j]
        cex[12:16, lane] = ch[8 + j]
    v = cex[...]
    w = v + fp[2]
    ends = [(v - tx[...]) * inv[...], w]
    a1 = stencils(wn, ends)
    a2 = stencils(wn, a1)
    a3 = [mid(v) for v in stencils(wn, a2)]
    ends = [mid(v) for v in ends]
    a1 = [mid(v) for v in a1]
    a2 = [mid(v) for v in a2]
    ends.append(dec * ends[1] + fp[1, own])
    for b in range(2):
        e, p1, p2, p3 = ends[b], a1[b], a2[b], a3[b]
        k = 8 * b
        ob[k] += e + p1
        ob[k + 1] += e + 2.0 * p1
        ob[k + 2] += e + 3.0 * p1 + 2.0 * p2
        ob[k + 3] += e + 4.0 * p1
        ob[k + 4] += e + 5.0 * p1 + 4.0 * p2
        ob[k + 5] += e + 6.0 * p1 + 8.0 * p2
        ob[k + 6] += e + 7.0 * p1 + 14.0 * p2 + 8.0 * p3
        ob[k + 7] += ends[b + 1]

    for cp in gather:
        cp.total.wait_send()


def body(slabs, strips, u_coarse_guess, forcing, u_init, diffuse, vel_x, vel_y, react):
    points, rows, cols = u_coarse_guess.shape
    wide = rows + 2 * PAD
    around = rows + 2 * NEAR
    copies = 4 + 4 + 3 + 3 + 2 + 10 + 3 + 2 + 3 + 1 + 2 + 2
    f32 = jnp.float32

    def vmem(*shape):
        return pltpu.VMEM(shape, f32)

    return pl.pallas_call(
        functools.partial(kernel, slabs, strips),
        out_shape=pltpu.VMEM(forcing.shape, f32),
        in_specs=[pl.BlockSpec(memory_space=pltpu.HBM)] * 7,
        out_specs=pl.BlockSpec(memory_space=pltpu.VMEM),
        scratch_shapes=[
            vmem(points + 1, around, cols),
            vmem(points, around, cols),
            vmem(points, rows, cols),
            vmem(4, rows, cols),
            vmem(4, rows, cols),
            vmem(4, rows, cols),
            vmem(5, wide, cols),
            vmem(5, around, cols),
            vmem(around, cols),
            vmem(3, around, cols),
            vmem(wide, cols),
            vmem(3, DEPTH + 1, rows, cols),
            vmem(points + 1, around, cols),
            vmem(points + 1, around, cols),
            vmem(3, wide, cols),
            vmem(2, 3, rows, cols),
            vmem(3, around, cols),
            vmem(around, cols),
            vmem(rows, cols),
            vmem(rows, cols),
            vmem(rows, cols),
            vmem(3, GROUP, 4, 128),
            vmem(GROUP, 4, 128),
            vmem(3, GROUP, 4, 128),
            vmem(GROUP, 4, 128),
            vmem(GROUP, 4, 128),
            vmem(slabs, 4, 128),
            vmem(GROUP, 4, 128),
            vmem(GROUP, 4, 128),
            vmem(GROUP, 4, 128),
            vmem(around, cols),
            pltpu.SemaphoreType.DMA((8,)),
            pltpu.SemaphoreType.DMA((copies,)),
            pltpu.SemaphoreType.DMA((copies,)),
            pltpu.SemaphoreType.REGULAR,
        ],
        compiler_params=pltpu.CompilerParams(
            collective_id=0, has_side_effects=True, vmem_limit_bytes=60 << 20
        ),
        cost_estimate=pl.CostEstimate(flops=10_000_000, bytes_accessed=1_500_000, transcendentals=16384),
    )(
        u_coarse_guess,
        forcing.reshape(points, 2, rows, cols),
        u_init,
        diffuse,
        vel_x,
        vel_y,
        react,
    )


def solution(mesh):
    slabs = mesh.shape["tm"] // GROUP
    strips = mesh.shape["space"]
    whole = P("tm", "space", None)
    row = P("space", None)
    return jax.shard_map(
        functools.partial(body, slabs, strips),
        mesh=mesh,
        in_specs=(whole, whole) + (row,) * 5,
        out_specs=whole,
        check_vma=False,
    )
```

```python
import functools

import jax
import jax.numpy as jnp
from jax import lax
from jax.experimental import pallas as pl
from jax.experimental.pallas import tpu as pltpu
from jax.sharding import PartitionSpec as P

MESH = pl.DeviceIdType.MESH
GROUP = 16
PAD = 8
NEAR = 4
DEPTH = 6


def add_squares(x):
    out = []
    for m in range(len(x) + 2):
        terms = []
        if m < len(x):
            terms.append(x[m])
        if 1 <= m <= len(x):
            terms.append(2.0 * x[m - 1])
        if 2 <= m <= len(x) + 1:
            terms.append(x[m - 2])
        total = terms[0]
        for t in terms[1:]:
            total = total + t
        out.append(total)
    return out


def kernel(
    slabs,
    strips,
    guess,
    force,
    init,
    diffuse,
    vel_x,
    vel_y,
    react,
    ob,
    gx,
    fx,
    hx,
    cx,
    cb,
    cn,
    cf,
    wx,
    wn,
    inv,
    rn,
    decx,
    px,
    dx,
    zx,
    rx,
    qx,
    fp,
    tx,
    ini,
    g7,
    d7,
    sp,
    dp,
    r1,
    pre,
    pw,
    r2,
    wo,
    ce,
    ch,
    cex,
    lsem,
    ss,
    sr,
    known,
):
    tm = lax.axis_index("tm")
    sx = lax.axis_index("space")
    y = tm // GROUP
    q = lax.rem(tm, GROUP)
    count = slabs * GROUP
    xs = (lax.rem(sx + 1, strips), lax.rem(sx + strips - 1, strips))
    nxt = lax.rem(tm + 1, count)
    prv = lax.rem(tm + count - 1, count)
    last = tm == count - 1
    cols = ob.shape[2]
    own = pl.ds(0, 8)
    centre_rows = pl.ds(PAD, 8)

    zc = q // 2
    core = lax.rem(q, 2)
    depth = GROUP // 2

    def along_z(m, c):
        return y * GROUP + lax.rem(zc + m + depth, depth) * 2 + c

    def along_y(m):
        return lax.rem(y + m + slabs, slabs) * GROUP + q

    barrier = pltpu.get_barrier_semaphore()
    peers = [(tm, s) for s in xs] + [(nxt, sx), (prv, sx)]
    for s in (sx,) + xs:
        peers.append((along_z(0, 1 - core), s))
        for m in (-2, -1, 1, 2):
            peers += [(along_z(m, 0), s), (along_z(m, 1), s)]
    for m in (-2, -1, 1, 2):
        peers.append((along_y(m), sx))
    for dev in peers:
        pl.semaphore_signal(barrier, inc=1, device_id=dev, device_id_type=MESH)

    loads = []
    for i, (src, dst) in enumerate(
        [
            (guess, gx.at[pl.ds(1, 8), own]),
            (force.at[:, 0], fx.at[:, own]),
            (force.at[:, 1], hx),
            (init, ini),
            (diffuse, cx.at[0]),
            (vel_x, cx.at[1]),
            (vel_y, cx.at[2]),
            (react, cx.at[3]),
        ]
    ):
        cp = pltpu.make_async_copy(src, dst, lsem.at[i])
        cp.start()
        loads.append(cp)
    for cp in loads:
        cp.wait()

    sent = []
    slot = [0]

    def send(src, dst, dev):
        i = slot[0]
        slot[0] += 1
        cp = pltpu.make_async_remote_copy(
            src_ref=src,
            dst_ref=dst,
            send_sem=ss.at[i],
            recv_sem=sr.at[i],
            device_id=dev,
            device_id_type=MESH,
        )
        cp.start()
        sent.append(cp)
        return cp

    class Batch:
        def __init__(self, items, whole):
            i = slot[0]
            slot[0] += 1
            for src, dst, dev in items:
                self.copy = pltpu.make_async_remote_copy(
                    src_ref=src,
                    dst_ref=dst,
                    send_sem=ss.at[i],
                    recv_sem=sr.at[i],
                    device_id=dev,
                    device_id_type=MESH,
                )
                self.copy.start()
            self.total = pltpu.make_async_remote_copy(
                src_ref=whole,
                dst_ref=whole,
                send_sem=ss.at[i],
                recv_sem=sr.at[i],
                device_id=items[0][2],
                device_id_type=MESH,
            )
            sent.append(self.total)

        def wait_recv(self):
            self.total.wait_recv()

    def far_first(n):
        return sorted(range(1, n), key=lambda m: -min(m, n - m))

    def halo(ref, lead, h):
        a = send(ref.at[lead + (pl.ds(8 - h, h),)], ref.at[lead + (pl.ds(16 - h, h),)], (tm, xs[0]))
        b = send(ref.at[lead + (pl.ds(0, h),)], ref.at[lead + (pl.ds(8, h),)], (tm, xs[1]))
        return [a, b]

    def onward(src, ref, lead, h):
        return [
            send(src, ref.at[lead + (own,)], (nxt, sx)),
            send(src.at[pl.ds(8 - h, h)], ref.at[lead + (pl.ds(16 - h, h),)], (nxt, xs[0])),
            send(src.at[pl.ds(0, h)], ref.at[lead + (pl.ds(8, h),)], (nxt, xs[1])),
        ]

    def change(G, F, H, k):
        return (G[k - 1] + F[k] + H[k] - G[k], 2.0 * G[k - 1] + F[k], G[k - 1])

    def reader(ref, lane, shift, padded):
        def read(k):
            if padded:
                return ref[k + shift, own, lane]
            return ref[k + shift, :, lane]

        class Reader:
            def __getitem__(self, k):
                return read(k)

        return Reader()

    def fields(lane):
        return reader(gx, lane, 1, True), reader(fx, lane, 0, True), reader(hx, lane, 0, False)

    def first(lane):
        G, F, H = fields(lane)
        d0, d1, d2 = [jnp.where(last, 0.0, v) for v in change(G, F, H, 7)]
        g = jnp.where(last, ini[:, lane], G[7])
        g7[:, lane] = g
        return [
            d0 + g,
            d1 + 6.0 * (d0 + g),
            d2 + 6.0 * d1 + 8.0 * d0 + 9.0 * g,
            6.0 * d2 + 8.0 * d1 + 4.0 * g,
            8.0 * d2,
        ]

    def second(lane):
        G, F, H = fields(lane)
        a0, a1, a2 = change(G, F, H, 3)
        b0, b1, b2 = change(G, F, H, 4)
        c0, c1, c2 = change(G, F, H, 5)
        e0, e1, e2 = change(G, F, H, 6)
        return [
            a0 + b0 + c0 + e0,
            a1 + 6.0 * a0 + b1 + 4.0 * b0 + c1 + 2.0 * c0 + e1,
            a2 + 6.0 * a1 + 8.0 * a0 + b2 + 4.0 * b1 + c2 + 2.0 * c1 + e2,
            6.0 * a2 + 8.0 * a1 + 4.0 * b2 + 2.0 * c2,
            8.0 * a2,
        ]

    def third(lane):
        G, F, H = fields(lane)
        b1 = F[0]
        b0 = b1 + H[0] - G[0]
        c0, c1, c2 = change(G, F, H, 1)
        e0, e1, e2 = change(G, F, H, 2)
        return [
            b0 + c0 + e0,
            b1 + 4.0 * b0 + c1 + 2.0 * c0 + e1,
            4.0 * b1 + c2 + 2.0 * c1 + e2,
            2.0 * c2,
        ]

    def combine(p, make):
        def one(j, carry):
            lane = pl.ds(pl.multiple_of(j * 128, 128), 128)
            for m, v in enumerate(add_squares(make(lane))):
                px[p, m, :, lane] = v
            return carry

        lax.fori_loop(0, cols // 128, one, 0)

    pl.semaphore_wait(barrier, len(peers))
    word = [along_z(-2, core), along_z(2, core), along_y(-2), along_y(2), prv]
    for dev in word:
        pl.semaphore_signal(known, inc=1, device_id=(dev, sx), device_id_type=MESH)

    def parameters(dst, up, down, n):
        return [
            send(cx.at[:, pl.ds(up, n)], dst.at[:, pl.ds(up, n)], (tm, xs[0])),
            send(cx.at[:, pl.ds(down, n)], dst.at[:, pl.ds(down, n)], (tm, xs[1])),
        ]

    closest = parameters(cb, 6, 0, 2)
    near = parameters(cn, 4, 2, 2)
    far = parameters(cf, 8 - DEPTH, NEAR, DEPTH - NEAR)
    early = halo(gx, (pl.ds(1, 7),), 2) + halo(fx, (slice(None),), 1)
    combine(0, first)
    combine(1, second)
    combine(2, third)

    row = lax.broadcasted_iota(jnp.int32, (8, cols), 0)
    col = lax.broadcasted_iota(jnp.int32, (8, cols), 1)
    low = row < NEAR
    above = sx > 0
    beneath = sx < strips - 1

    def weights(raw, inside, top, bottom):
        dif, vx, vy, rea = raw
        west = jnp.where(col == 0, 0.0, dif + jnp.maximum(vx, 0.0))
        east = jnp.where(col == cols - 1, 0.0, dif - jnp.minimum(vx, 0.0))
        north = dif + jnp.maximum(vy, 0.0)
        south = dif - jnp.minimum(vy, 0.0)
        centre = -(4.0 * dif + jnp.abs(vx) + jnp.abs(vy) + rea)
        if inside is not None:
            return [jnp.where(inside, v, 0.0) for v in (west, east, north, south, centre)]
        return [west, east, jnp.where(top, 0.0, north), jnp.where(bottom, 0.0, south), centre]

    raw = [cx[i] for i in range(4)]
    edge = weights(raw, None, (row == 0) & (sx == 0), (row == 7) & (sx == strips - 1))
    for i, v in enumerate(edge):
        wx[i, 8:16] = v
        wn[i, 0:8] = v
    decx[8:16] = jnp.exp(-8.0 * raw[3])
    inv[0:8] = jnp.exp(8.0 * raw[3])

    for cp in closest:
        cp.wait_recv()
    beside = (low & beneath) | (~low & above)
    two = (row < 2) | (row >= 6)
    raw = [cb[i] for i in range(4)]
    for i, v in enumerate(weights(raw, beside & two, None, None)):
        wn[i, 8:16] = v

    def stencils(w, values):
        n = values[0].shape[0]
        total = [w[4] * v for v in values]
        for i, shift, axis in ((0, 1, 1), (1, cols - 1, 1), (2, 1, 0), (3, n - 1, 0)):
            weight = w[i]
            total = [t + weight * pltpu.roll(v, shift, axis) for t, v in zip(total, values)]
        return total

    def stencil(w, v):
        return stencils(w, [v])[0]

    def ap(v):
        return stencil(wn, v)

    def mid(v):
        return v[0:8]

    def around(v):
        none = jnp.zeros_like(v)
        return jnp.concatenate([none, v, none], axis=0)

    tops = (DEPTH, DEPTH, DEPTH - 1)

    def start(p, m):
        v = px[p, m]
        return jnp.concatenate([v, jnp.zeros_like(v)], axis=0)

    for p in range(3):
        rn[p] = start(p, tops[p])

    def level_near(i, carry):
        new = stencils(wn, [rn[p] for p in range(3)])
        for p in range(3):
            rn[p] = new[p] + start(p, tops[p] - 1 - i)
        return carry

    lax.fori_loop(0, 2, level_near, 0)
    for cp in near:
        cp.wait_recv()
    four = [jnp.where(two, cb[i], cn[i]) for i in range(4)]
    for i, v in enumerate(weights(four, beside, None, None)):
        wn[i, 8:16] = v
    lax.fori_loop(2, NEAR, level_near, 0)

    for cp in far:
        cp.wait_recv()
    for t, inside in ((0, (row >= PAD - DEPTH) & above), (2, (row < DEPTH) & beneath)):
        raw = [jnp.where(low, four[i] if t else cf[i], cf[i] if t else four[i]) for i in range(4)]
        for i, v in enumerate(weights(raw, inside, None, None)):
            wx[i, 8 * t : 8 * t + 8] = v
        decx[8 * t : 8 * t + 8] = jnp.where(inside, jnp.exp(-8.0 * raw[3]), 0.0)

    for p in range(3):
        v = rn[p, 8:16]
        rx[p] = jnp.concatenate([jnp.where(low, 0.0, v), rn[p, 0:8], jnp.where(low, v, 0.0)], axis=0)
    for i in range(NEAR, DEPTH):
        left = [p for p in range(3) if i < tops[p]]
        new = stencils(wx, [rx[p] for p in left])
        for p in left:
            rx[p] = new[p] + around(px[p, tops[p] - 1 - i])

    decv = decx[...]
    dec = decv[8:16]
    value = rx[0]
    part = jnp.where(last, value, decv * (decv * rx[2] + rx[1]) + value)
    for h in (0, 1):
        for j in range(8):
            dp[8 * h + j] = dec[4 * h : 4 * h + 4, 128 * j : 128 * j + 128]
            for t in range(3):
                r = 8 * t + 4 * h
                sp[t, 8 * h + j] = part[r : r + 4, 128 * j : 128 * j + 128]

    pl.semaphore_wait(known, len(word))

    def mate(m):
        to = lax.rem(q + m, GROUP)
        return to, y * GROUP + to

    items = ([], [], [])
    for m in far_first(GROUP) + [0]:
        to, dev = mate(m)
        items[2].append((sp.at[2, to], r1.at[2, q], (dev, xs[0])))
        items[0].append((sp.at[0, to], r1.at[0, q], (dev, xs[1])))
        if m:
            items[1].append((sp.at[1, to], r1.at[1, q], (dev, sx)))
    scatter = [Batch(items[2], r1.at[2]), Batch(items[0], r1.at[0]), Batch(items[1], r1.at[1, pl.ds(0, GROUP - 1)])]
    r1[1, q] = sp[1, q]
    spill = [
        send(rx.at[:, pl.ds(16, DEPTH)], qx.at[0, :, pl.ds(0, DEPTH)], (tm, xs[0])),
        send(rx.at[:, pl.ds(8 - DEPTH, DEPTH)], qx.at[1, :, pl.ds(8 - DEPTH, DEPTH)], (tm, xs[1])),
    ]
    early += onward(g7, gx, (0,), 2)
    inv[8:16] = jnp.exp(8.0 * four[3])
    d1 = dp[q]
    d2 = d1 * d1

    for cp in early:
        cp.wait_recv()

    def changes(k, carry):
        g, f = gx[k], fx[k]
        v = ap(g) + 2.0 * g + f
        dx[k + 1, own] = mid(ap(v)) + mid(g + f) + hx[k] - gx[k + 1, own]
        return carry

    lax.fori_loop(0, 8, changes, 0)
    d7[...] = jnp.where(last, 0.0, dx[8, own])
    middle = []
    for k, h in ((0, 3), (1, 2), (3, 4), (4, 3), (5, 2)):
        middle += halo(dx, (k + 1,), h)
    middle += onward(d7, dx, (0,), 4)
    for cp in spill:
        cp.wait_recv()
    for p in range(3):
        over = jnp.where(row < DEPTH, qx[0, p], 0.0)
        under = jnp.where(row >= 8 - DEPTH, qx[1, p], 0.0)
        fp[p, own] = rx[p, centre_rows] + over + under
    late = halo(fp, (2,), 3) + onward(fp.at[0, own], tx, (), 3)

    for cp in scatter:
        cp.wait_recv()
    acc = jnp.zeros_like(d2)
    fac = jnp.ones_like(d2)
    for i in range(GROUP):
        pre[i] = acc
        pw[i] = fac
        part = r1[1, i] + r1[2, i] + r1[0, i]
        acc = d2 * acc + part
        fac = d2 * fac
    r2[y] = jnp.where(y == slabs - 1, part, acc)
    items = []
    for m in far_first(slabs):
        items.append((r2.at[y], r2.at[y], (lax.rem(y + m, slabs) * GROUP + q, sx)))
    across = [Batch(items, r2.at[pl.ds(0, slabs - 1)])]

    for cp in middle:
        cp.wait_recv()
    zx[0] = gx[0] + dx[0]

    def twice(v):
        v = v + ap(v)
        return mid(v) + mid(ap(v))

    def blocks(b, carry):
        k = 4 * b
        a = dx[k]
        bb = dx[k + 1]
        c = dx[k + 2]
        zx[k + 1, own] = gx[k + 1, own] + mid(bb) + twice(a)
        w = a + 2.0 * ap(a) + bb
        zx[k + 2, own] = gx[k + 2, own] + mid(c) + twice(w)
        w = w + 2.0 * ap(w) + c
        zx[k + 3, own] = gx[k + 3, own] + dx[k + 3, own] + twice(w)
        zx[k + 4, own] = gx[k + 4, own] + dx[k + 4, own]
        return carry

    lax.fori_loop(0, 2, blocks, 0)
    coarse = halo(zx, (pl.ds(1, 7),), 1)

    for cp in across:
        cp.wait_recv()
    acc = r2[slabs - 1]
    for i in range(slabs - 1):
        acc = jnp.where(i < y, fac * acc + r2[i], acc)
    for i in range(GROUP):
        wo[i] = pw[i] * acc + pre[i]
    half = q // 8
    side = lax.rem(sx + 2 * half + strips - 1, strips)
    items = ([], [])
    for m in far_first(GROUP) + [0]:
        to, dev = mate(m)
        items[0].append((wo.at[to], ch.at[q], (dev, side)))
        if m:
            items[1].append((wo.at[to], ce.at[q], (dev, sx)))
    early_sent = list(sent)
    gather = [Batch(items[0], ch), Batch(items[1], ce.at[pl.ds(0, GROUP - 1)])]
    ce[q] = wo[q]

    for cp in coarse:
        cp.wait_recv()

    def results(k, carry):
        v = zx[k]
        ob[2 * k] = mid(v) + mid(ap(v)) + fx[k, own]
        ob[2 * k + 1] = zx[k + 1, own]
        return carry

    lax.fori_loop(0, 8, results, 0)
    for cp in late:
        cp.wait_recv()
    for cp in early_sent:
        cp.wait_send()

    for cp in gather:
        cp.wait_recv()
    for j in range(8):
        lane = pl.ds(128 * j, 128)
        cex[0:4, lane] = ce[j]
        cex[4:8, lane] = ce[8 + j]
        cex[8:12, lane] = ch[j]
        cex[12:16, lane] = ch[8 + j]
    v = cex[...]
    w = v + fp[2]
    ends = [(v - tx[...]) * inv[...], w]
    a1 = stencils(wn, ends)
    a2 = stencils(wn, a1)
    a3 = [mid(v) for v in stencils(wn, a2)]
    ends = [mid(v) for v in ends]
    a1 = [mid(v) for v in a1]
    a2 = [mid(v) for v in a2]
    ends.append(dec * ends[1] + fp[1, own])
    for b in range(2):
        e, p1, p2, p3 = ends[b], a1[b], a2[b], a3[b]
        k = 8 * b
        ob[k] += e + p1
        ob[k + 1] += e + 2.0 * p1
        ob[k + 2] += e + 3.0 * p1 + 2.0 * p2
        ob[k + 3] += e + 4.0 * p1
        ob[k + 4] += e + 5.0 * p1 + 4.0 * p2
        ob[k + 5] += e + 6.0 * p1 + 8.0 * p2
        ob[k + 6] += e + 7.0 * p1 + 14.0 * p2 + 8.0 * p3
        ob[k + 7] += ends[b + 1]

    for cp in gather:
        cp.total.wait_send()


def body(slabs, strips, u_coarse_guess, forcing, u_init, diffuse, vel_x, vel_y, react):
    points, rows, cols = u_coarse_guess.shape
    wide = rows + 2 * PAD
    around = rows + 2 * NEAR
    copies = 6 + 4 + 3 + 3 + 2 + 10 + 3 + 2 + 3 + 1 + 2 + 2
    f32 = jnp.float32

    def vmem(*shape):
        return pltpu.VMEM(shape, f32)

    return pl.pallas_call(
        functools.partial(kernel, slabs, strips),
        out_shape=pltpu.VMEM(forcing.shape, f32),
        in_specs=[pl.BlockSpec(memory_space=pltpu.HBM)] * 7,
        out_specs=pl.BlockSpec(memory_space=pltpu.VMEM),
        scratch_shapes=[
            vmem(points + 1, around, cols),
            vmem(points, around, cols),
            vmem(points, rows, cols),
            vmem(4, rows, cols),
            vmem(4, rows, cols),
            vmem(4, rows, cols),
            vmem(4, rows, cols),
            vmem(5, wide, cols),
            vmem(5, around, cols),
            vmem(around, cols),
            vmem(3, around, cols),
            vmem(wide, cols),
            vmem(3, DEPTH + 1, rows, cols),
            vmem(points + 1, around, cols),
            vmem(points + 1, around, cols),
            vmem(3, wide, cols),
            vmem(2, 3, rows, cols),
            vmem(3, around, cols),
            vmem(around, cols),
            vmem(rows, cols),
            vmem(rows, cols),
            vmem(rows, cols),
            vmem(3, GROUP, 4, 128),
            vmem(GROUP, 4, 128),
            vmem(3, GROUP, 4, 128),
            vmem(GROUP, 4, 128),
            vmem(GROUP, 4, 128),
            vmem(slabs, 4, 128),
            vmem(GROUP, 4, 128),
            vmem(GROUP, 4, 128),
            vmem(GROUP, 4, 128),
            vmem(around, cols),
            pltpu.SemaphoreType.DMA((8,)),
            pltpu.SemaphoreType.DMA((copies,)),
            pltpu.SemaphoreType.DMA((copies,)),
            pltpu.SemaphoreType.REGULAR,
        ],
        compiler_params=pltpu.CompilerParams(
            collective_id=0, has_side_effects=True, vmem_limit_bytes=60 << 20
        ),
        cost_estimate=pl.CostEstimate(flops=10_000_000, bytes_accessed=1_500_000, transcendentals=16384),
    )(
        u_coarse_guess,
        forcing.reshape(points, 2, rows, cols),
        u_init,
        diffuse,
        vel_x,
        vel_y,
        react,
    )


def solution(mesh):
    slabs = mesh.shape["tm"] // GROUP
    strips = mesh.shape["space"]
    whole = P("tm", "space", None)
    row = P("space", None)
    return jax.shard_map(
        functools.partial(body, slabs, strips),
        mesh=mesh,
        in_specs=(whole, whole) + (row,) * 5,
        out_specs=whole,
        check_vma=False,
    )
```

```python
import functools

import jax
import jax.numpy as jnp
from jax import lax
from jax.experimental import pallas as pl
from jax.experimental.pallas import tpu as pltpu
from jax.sharding import PartitionSpec as P

MESH = pl.DeviceIdType.MESH
GROUP = 16
PAD = 8
NEAR = 4
DEPTH = 6


def add_squares(x):
    out = []
    for m in range(len(x) + 2):
        terms = []
        if m < len(x):
            terms.append(x[m])
        if 1 <= m <= len(x):
            terms.append(2.0 * x[m - 1])
        if 2 <= m <= len(x) + 1:
            terms.append(x[m - 2])
        total = terms[0]
        for t in terms[1:]:
            total = total + t
        out.append(total)
    return out


def kernel(
    slabs,
    strips,
    guess,
    force,
    init,
    diffuse,
    vel_x,
    vel_y,
    react,
    ob,
    gx,
    fx,
    hx,
    cx,
    cb,
    cn,
    cf,
    wx,
    wn,
    inv,
    rn,
    decx,
    px,
    dx,
    zx,
    rx,
    qx,
    fp,
    tx,
    ini,
    g7,
    d7,
    sp,
    dp,
    r1,
    pre,
    pw,
    r2,
    wo,
    ce,
    ch,
    cex,
    lsem,
    ss,
    sr,
    known,
):
    tm = lax.axis_index("tm")
    sx = lax.axis_index("space")
    y = tm // GROUP
    q = lax.rem(tm, GROUP)
    count = slabs * GROUP
    xs = (lax.rem(sx + 1, strips), lax.rem(sx + strips - 1, strips))
    nxt = lax.rem(tm + 1, count)
    prv = lax.rem(tm + count - 1, count)
    last = tm == count - 1
    cols = ob.shape[2]
    own = pl.ds(0, 8)
    centre_rows = pl.ds(PAD, 8)

    zc = q // 2
    core = lax.rem(q, 2)
    depth = GROUP // 2

    def along_z(m, c):
        return y * GROUP + lax.rem(zc + m + depth, depth) * 2 + c

    def along_y(m):
        return lax.rem(y + m + slabs, slabs) * GROUP + q

    barrier = pltpu.get_barrier_semaphore()
    peers = [(tm, s) for s in xs] + [(nxt, sx), (prv, sx)]
    for s in (sx,) + xs:
        peers.append((along_z(0, 1 - core), s))
        for m in (-2, -1, 1, 2):
            peers += [(along_z(m, 0), s), (along_z(m, 1), s)]
    for m in (-2, -1, 1, 2):
        peers.append((along_y(m), sx))
    for dev in peers:
        pl.semaphore_signal(barrier, inc=1, device_id=dev, device_id_type=MESH)

    loads = []
    for i, (src, dst) in enumerate(
        [
            (guess, gx.at[pl.ds(1, 8), own]),
            (force.at[:, 0], fx.at[:, own]),
            (force.at[:, 1], hx),
            (init, ini),
            (diffuse, cx.at[0]),
            (vel_x, cx.at[1]),
            (vel_y, cx.at[2]),
            (react, cx.at[3]),
        ]
    ):
        cp = pltpu.make_async_copy(src, dst, lsem.at[i])
        cp.start()
        loads.append(cp)
    for cp in loads:
        cp.wait()

    sent = []
    slot = [0]

    def send(src, dst, dev):
        i = slot[0]
        slot[0] += 1
        cp = pltpu.make_async_remote_copy(
            src_ref=src,
            dst_ref=dst,
            send_sem=ss.at[i],
            recv_sem=sr.at[i],
            device_id=dev,
            device_id_type=MESH,
        )
        cp.start()
        sent.append(cp)
        return cp

    class Batch:
        def __init__(self, items, whole):
            i = slot[0]
            slot[0] += 1
            for src, dst, dev in items:
                self.copy = pltpu.make_async_remote_copy(
                    src_ref=src,
                    dst_ref=dst,
                    send_sem=ss.at[i],
                    recv_sem=sr.at[i],
                    device_id=dev,
                    device_id_type=MESH,
                )
                self.copy.start()
            self.total = pltpu.make_async_remote_copy(
                src_ref=whole,
                dst_ref=whole,
                send_sem=ss.at[i],
                recv_sem=sr.at[i],
                device_id=items[0][2],
                device_id_type=MESH,
            )
            sent.append(self.total)

        def wait_recv(self):
            self.total.wait_recv()

    def far_first(n):
        return sorted(range(1, n), key=lambda m: -min(m, n - m))

    def halo(ref, lead, h):
        a = send(ref.at[lead + (pl.ds(8 - h, h),)], ref.at[lead + (pl.ds(16 - h, h),)], (tm, xs[0]))
        b = send(ref.at[lead + (pl.ds(0, h),)], ref.at[lead + (pl.ds(8, h),)], (tm, xs[1]))
        return [a, b]

    def onward(src, ref, lead, h):
        return [
            send(src, ref.at[lead + (own,)], (nxt, sx)),
            send(src.at[pl.ds(8 - h, h)], ref.at[lead + (pl.ds(16 - h, h),)], (nxt, xs[0])),
            send(src.at[pl.ds(0, h)], ref.at[lead + (pl.ds(8, h),)], (nxt, xs[1])),
        ]

    def change(G, F, H, k):
        return (G[k - 1] + F[k] + H[k] - G[k], 2.0 * G[k - 1] + F[k], G[k - 1])

    def reader(ref, lane, shift, padded):
        def read(k):
            if padded:
                return ref[k + shift, own, lane]
            return ref[k + shift, :, lane]

        class Reader:
            def __getitem__(self, k):
                return read(k)

        return Reader()

    def fields(lane):
        return reader(gx, lane, 1, True), reader(fx, lane, 0, True), reader(hx, lane, 0, False)

    def first(lane):
        G, F, H = fields(lane)
        d0, d1, d2 = [jnp.where(last, 0.0, v) for v in change(G, F, H, 7)]
        g = jnp.where(last, ini[:, lane], G[7])
        g7[:, lane] = g
        return [
            d0 + g,
            d1 + 6.0 * (d0 + g),
            d2 + 6.0 * d1 + 8.0 * d0 + 9.0 * g,
            6.0 * d2 + 8.0 * d1 + 4.0 * g,
            8.0 * d2,
        ]

    def second(lane):
        G, F, H = fields(lane)
        a0, a1, a2 = change(G, F, H, 3)
        b0, b1, b2 = change(G, F, H, 4)
        c0, c1, c2 = change(G, F, H, 5)
        e0, e1, e2 = change(G, F, H, 6)
        return [
            a0 + b0 + c0 + e0,
            a1 + 6.0 * a0 + b1 + 4.0 * b0 + c1 + 2.0 * c0 + e1,
            a2 + 6.0 * a1 + 8.0 * a0 + b2 + 4.0 * b1 + c2 + 2.0 * c1 + e2,
            6.0 * a2 + 8.0 * a1 + 4.0 * b2 + 2.0 * c2,
            8.0 * a2,
        ]

    def third(lane):
        G, F, H = fields(lane)
        b1 = F[0]
        b0 = b1 + H[0] - G[0]
        c0, c1, c2 = change(G, F, H, 1)
        e0, e1, e2 = change(G, F, H, 2)
        return [
            b0 + c0 + e0,
            b1 + 4.0 * b0 + c1 + 2.0 * c0 + e1,
            4.0 * b1 + c2 + 2.0 * c1 + e2,
            2.0 * c2,
        ]

    def combine(p, make):
        def one(j, carry):
            lane = pl.ds(pl.multiple_of(j * 128, 128), 128)
            for m, v in enumerate(add_squares(make(lane))):
                px[p, m, :, lane] = v
            return carry

        lax.fori_loop(0, cols // 128, one, 0)

    combine(0, first)
    combine(1, second)
    combine(2, third)
    pl.semaphore_wait(barrier, len(peers))
    word = [along_z(-2, core), along_z(2, core), along_y(-2), along_y(2), prv]
    for dev in word:
        pl.semaphore_signal(known, inc=1, device_id=(dev, sx), device_id_type=MESH)

    def parameters(dst, up, down, n):
        return [
            send(cx.at[:, pl.ds(up, n)], dst.at[:, pl.ds(up, n)], (tm, xs[0])),
            send(cx.at[:, pl.ds(down, n)], dst.at[:, pl.ds(down, n)], (tm, xs[1])),
        ]

    closest = parameters(cb, 6, 0, 2)
    near = parameters(cn, 4, 2, 2)
    far = parameters(cf, 8 - DEPTH, NEAR, DEPTH - NEAR)
    early = halo(gx, (pl.ds(1, 7),), 2) + halo(fx, (slice(None),), 1)

    row = lax.broadcasted_iota(jnp.int32, (8, cols), 0)
    col = lax.broadcasted_iota(jnp.int32, (8, cols), 1)
    low = row < NEAR
    above = sx > 0
    beneath = sx < strips - 1

    def weights(raw, inside, top, bottom):
        dif, vx, vy, rea = raw
        west = jnp.where(col == 0, 0.0, dif + jnp.maximum(vx, 0.0))
        east = jnp.where(col == cols - 1, 0.0, dif - jnp.minimum(vx, 0.0))
        north = dif + jnp.maximum(vy, 0.0)
        south = dif - jnp.minimum(vy, 0.0)
        centre = -(4.0 * dif + jnp.abs(vx) + jnp.abs(vy) + rea)
        if inside is not None:
            return [jnp.where(inside, v, 0.0) for v in (west, east, north, south, centre)]
        return [west, east, jnp.where(top, 0.0, north), jnp.where(bottom, 0.0, south), centre]

    raw = [cx[i] for i in range(4)]
    edge = weights(raw, None, (row == 0) & (sx == 0), (row == 7) & (sx == strips - 1))
    for i, v in enumerate(edge):
        wx[i, 8:16] = v
        wn[i, 0:8] = v
    decx[8:16] = jnp.exp(-8.0 * raw[3])
    inv[0:8] = jnp.exp(8.0 * raw[3])

    for cp in closest:
        cp.wait_recv()
    beside = (low & beneath) | (~low & above)
    two = (row < 2) | (row >= 6)
    raw = [cb[i] for i in range(4)]
    for i, v in enumerate(weights(raw, beside & two, None, None)):
        wn[i, 8:16] = v

    def stencils(w, values):
        n = values[0].shape[0]
        total = [w[4] * v for v in values]
        for i, shift, axis in ((0, 1, 1), (1, cols - 1, 1), (2, 1, 0), (3, n - 1, 0)):
            weight = w[i]
            total = [t + weight * pltpu.roll(v, shift, axis) for t, v in zip(total, values)]
        return total

    def stencil(w, v):
        return stencils(w, [v])[0]

    def ap(v):
        return stencil(wn, v)

    def mid(v):
        return v[0:8]

    def around(v):
        none = jnp.zeros_like(v)
        return jnp.concatenate([none, v, none], axis=0)

    tops = (DEPTH, DEPTH, DEPTH - 1)

    def start(p, m):
        v = px[p, m]
        return jnp.concatenate([v, jnp.zeros_like(v)], axis=0)

    for p in range(3):
        rn[p] = start(p, tops[p])

    def level_near(i, carry):
        new = stencils(wn, [rn[p] for p in range(3)])
        for p in range(3):
            rn[p] = new[p] + start(p, tops[p] - 1 - i)
        return carry

    lax.fori_loop(0, 2, level_near, 0)
    for cp in near:
        cp.wait_recv()
    four = [jnp.where(two, cb[i], cn[i]) for i in range(4)]
    for i, v in enumerate(weights(four, beside, None, None)):
        wn[i, 8:16] = v
    lax.fori_loop(2, NEAR, level_near, 0)

    for cp in far:
        cp.wait_recv()
    for t, inside in ((0, (row >= PAD - DEPTH) & above), (2, (row < DEPTH) & beneath)):
        raw = [jnp.where(low, four[i] if t else cf[i], cf[i] if t else four[i]) for i in range(4)]
        for i, v in enumerate(weights(raw, inside, None, None)):
            wx[i, 8 * t : 8 * t + 8] = v
        decx[8 * t : 8 * t + 8] = jnp.where(inside, jnp.exp(-8.0 * raw[3]), 0.0)

    for p in range(3):
        v = rn[p, 8:16]
        rx[p] = jnp.concatenate([jnp.where(low, 0.0, v), rn[p, 0:8], jnp.where(low, v, 0.0)], axis=0)
    for i in range(NEAR, DEPTH):
        left = [p for p in range(3) if i < tops[p]]
        new = stencils(wx, [rx[p] for p in left])
        for p in left:
            rx[p] = new[p] + around(px[p, tops[p] - 1 - i])

    decv = decx[...]
    dec = decv[8:16]
    value = rx[0]
    part = jnp.where(last, value, decv * (decv * rx[2] + rx[1]) + value)
    for h in (0, 1):
        for j in range(8):
            dp[8 * h + j] = dec[4 * h : 4 * h + 4, 128 * j : 128 * j + 128]
            for t in range(3):
                r = 8 * t + 4 * h
                sp[t, 8 * h + j] = part[r : r + 4, 128 * j : 128 * j + 128]

    pl.semaphore_wait(known, len(word))

    def mate(m):
        to = lax.rem(q + m, GROUP)
        return to, y * GROUP + to

    items = ([], [], [])
    for m in far_first(GROUP) + [0]:
        to, dev = mate(m)
        items[2].append((sp.at[2, to], r1.at[2, q], (dev, xs[0])))
        items[0].append((sp.at[0, to], r1.at[0, q], (dev, xs[1])))
        if m:
            items[1].append((sp.at[1, to], r1.at[1, q], (dev, sx)))
    scatter = [Batch(items[2], r1.at[2]), Batch(items[0], r1.at[0]), Batch(items[1], r1.at[1, pl.ds(0, GROUP - 1)])]
    r1[1, q] = sp[1, q]
    spill = [
        send(rx.at[:, pl.ds(16, DEPTH)], qx.at[0, :, pl.ds(0, DEPTH)], (tm, xs[0])),
        send(rx.at[:, pl.ds(8 - DEPTH, DEPTH)], qx.at[1, :, pl.ds(8 - DEPTH, DEPTH)], (tm, xs[1])),
    ]
    early += onward(g7, gx, (0,), 2)
    inv[8:16] = jnp.exp(8.0 * four[3])
    d1 = dp[q]
    d2 = d1 * d1

    for cp in early:
        cp.wait_recv()

    def changes(k, carry):
        g, f = gx[k], fx[k]
        v = ap(g) + 2.0 * g + f
        dx[k + 1, own] = mid(ap(v)) + mid(g + f) + hx[k] - gx[k + 1, own]
        return carry

    lax.fori_loop(0, 8, changes, 0)
    d7[...] = jnp.where(last, 0.0, dx[8, own])
    middle = []
    for k, h in ((0, 3), (1, 2), (3, 4), (4, 3), (5, 2)):
        middle += halo(dx, (k + 1,), h)
    middle += onward(d7, dx, (0,), 4)
    for cp in spill:
        cp.wait_recv()
    for p in range(3):
        over = jnp.where(row < DEPTH, qx[0, p], 0.0)
        under = jnp.where(row >= 8 - DEPTH, qx[1, p], 0.0)
        fp[p, own] = rx[p, centre_rows] + over + under
    late = halo(fp, (2,), 3) + onward(fp.at[0, own], tx, (), 3)

    for cp in scatter:
        cp.wait_recv()
    acc = jnp.zeros_like(d2)
    fac = jnp.ones_like(d2)
    for i in range(GROUP):
        pre[i] = acc
        pw[i] = fac
        part = r1[1, i] + r1[2, i] + r1[0, i]
        acc = d2 * acc + part
        fac = d2 * fac
    r2[y] = jnp.where(y == slabs - 1, part, acc)
    items = []
    for m in far_first(slabs):
        items.append((r2.at[y], r2.at[y], (lax.rem(y + m, slabs) * GROUP + q, sx)))
    across = [Batch(items, r2.at[pl.ds(0, slabs - 1)])]

    for cp in middle:
        cp.wait_recv()
    zx[0] = gx[0] + dx[0]

    def twice(v):
        v = v + ap(v)
        return mid(v) + mid(ap(v))

    def blocks(b, carry):
        k = 4 * b
        a = dx[k]
        bb = dx[k + 1]
        c = dx[k + 2]
        zx[k + 1, own] = gx[k + 1, own] + mid(bb) + twice(a)
        w = a + 2.0 * ap(a) + bb
        zx[k + 2, own] = gx[k + 2, own] + mid(c) + twice(w)
        w = w + 2.0 * ap(w) + c
        zx[k + 3, own] = gx[k + 3, own] + dx[k + 3, own] + twice(w)
        zx[k + 4, own] = gx[k + 4, own] + dx[k + 4, own]
        return carry

    lax.fori_loop(0, 2, blocks, 0)
    coarse = halo(zx, (pl.ds(1, 7),), 1)

    for cp in across:
        cp.wait_recv()
    acc = r2[slabs - 1]
    for i in range(slabs - 1):
        acc = jnp.where(i < y, fac * acc + r2[i], acc)
    for i in range(GROUP):
        wo[i] = pw[i] * acc + pre[i]
    half = q // 8
    side = lax.rem(sx + 2 * half + strips - 1, strips)
    items = ([], [])
    for m in far_first(GROUP) + [0]:
        to, dev = mate(m)
        items[0].append((wo.at[to], ch.at[q], (dev, side)))
        if m:
            items[1].append((wo.at[to], ce.at[q], (dev, sx)))
    early_sent = list(sent)
    gather = [Batch(items[0], ch), Batch(items[1], ce.at[pl.ds(0, GROUP - 1)])]
    ce[q] = wo[q]

    for cp in coarse:
        cp.wait_recv()

    def results(k, carry):
        v = zx[k]
        ob[2 * k] = mid(v) + mid(ap(v)) + fx[k, own]
        ob[2 * k + 1] = zx[k + 1, own]
        return carry

    lax.fori_loop(0, 8, results, 0)
    for cp in late:
        cp.wait_recv()
    for cp in early_sent:
        cp.wait_send()

    for cp in gather:
        cp.wait_recv()
    for j in range(8):
        lane = pl.ds(128 * j, 128)
        cex[0:4, lane] = ce[j]
        cex[4:8, lane] = ce[8 + j]
        cex[8:12, lane] = ch[j]
        cex[12:16, lane] = ch[8 + j]
    v = cex[...]
    w = v + fp[2]
    ends = [(v - tx[...]) * inv[...], w]
    a1 = stencils(wn, ends)
    a2 = stencils(wn, a1)
    a3 = [mid(v) for v in stencils(wn, a2)]
    ends = [mid(v) for v in ends]
    a1 = [mid(v) for v in a1]
    a2 = [mid(v) for v in a2]
    ends.append(dec * ends[1] + fp[1, own])
    for b in range(2):
        e, p1, p2, p3 = ends[b], a1[b], a2[b], a3[b]
        k = 8 * b
        ob[k] += e + p1
        ob[k + 1] += e + 2.0 * p1
        ob[k + 2] += e + 3.0 * p1 + 2.0 * p2
        ob[k + 3] += e + 4.0 * p1
        ob[k + 4] += e + 5.0 * p1 + 4.0 * p2
        ob[k + 5] += e + 6.0 * p1 + 8.0 * p2
        ob[k + 6] += e + 7.0 * p1 + 14.0 * p2 + 8.0 * p3
        ob[k + 7] += ends[b + 1]

    for cp in gather:
        cp.total.wait_send()


def body(slabs, strips, u_coarse_guess, forcing, u_init, diffuse, vel_x, vel_y, react):
    points, rows, cols = u_coarse_guess.shape
    wide = rows + 2 * PAD
    around = rows + 2 * NEAR
    copies = 6 + 4 + 3 + 3 + 2 + 10 + 3 + 2 + 3 + 1 + 2 + 2
    f32 = jnp.float32

    def vmem(*shape):
        return pltpu.VMEM(shape, f32)

    return pl.pallas_call(
        functools.partial(kernel, slabs, strips),
        out_shape=pltpu.VMEM(forcing.shape, f32),
        in_specs=[pl.BlockSpec(memory_space=pltpu.HBM)] * 7,
        out_specs=pl.BlockSpec(memory_space=pltpu.VMEM),
        scratch_shapes=[
            vmem(points + 1, around, cols),
            vmem(points, around, cols),
            vmem(points, rows, cols),
            vmem(4, rows, cols),
            vmem(4, rows, cols),
            vmem(4, rows, cols),
            vmem(4, rows, cols),
            vmem(5, wide, cols),
            vmem(5, around, cols),
            vmem(around, cols),
            vmem(3, around, cols),
            vmem(wide, cols),
            vmem(3, DEPTH + 1, rows, cols),
            vmem(points + 1, around, cols),
            vmem(points + 1, around, cols),
            vmem(3, wide, cols),
            vmem(2, 3, rows, cols),
            vmem(3, around, cols),
            vmem(around, cols),
            vmem(rows, cols),
            vmem(rows, cols),
            vmem(rows, cols),
            vmem(3, GROUP, 4, 128),
            vmem(GROUP, 4, 128),
            vmem(3, GROUP, 4, 128),
            vmem(GROUP, 4, 128),
            vmem(GROUP, 4, 128),
            vmem(slabs, 4, 128),
            vmem(GROUP, 4, 128),
            vmem(GROUP, 4, 128),
            vmem(GROUP, 4, 128),
            vmem(around, cols),
            pltpu.SemaphoreType.DMA((8,)),
            pltpu.SemaphoreType.DMA((copies,)),
            pltpu.SemaphoreType.DMA((copies,)),
            pltpu.SemaphoreType.REGULAR,
        ],
        compiler_params=pltpu.CompilerParams(
            collective_id=0, has_side_effects=True, vmem_limit_bytes=60 << 20
        ),
        cost_estimate=pl.CostEstimate(flops=10_000_000, bytes_accessed=1_500_000, transcendentals=16384),
    )(
        u_coarse_guess,
        forcing.reshape(points, 2, rows, cols),
        u_init,
        diffuse,
        vel_x,
        vel_y,
        react,
    )


def solution(mesh):
    slabs = mesh.shape["tm"] // GROUP
    strips = mesh.shape["space"]
    whole = P("tm", "space", None)
    row = P("space", None)
    return jax.shard_map(
        functools.partial(body, slabs, strips),
        mesh=mesh,
        in_specs=(whole, whole) + (row,) * 5,
        out_specs=whole,
        check_vma=False,
    )
```
